32 devices in a mesh: curve: 8 (over z, x), group: 4 (over y, core).
Axes of the slice: x: 2, y: 2, z: 4, core: 2. Of those that a mesh axis runs over, the one named last changes fastest.
Arguments:
- positions: float32 [4, 128, 3, 128], P('group', 'curve'), may hold values from 0 to 5.2, as said below
- velocities: float32 [4, 128, 3, 128], P('group', 'curve'), may hold values from -3 to 3
- masses: float32 [4, 128, 128], P('group', 'curve'), may hold values from 0.003 to 0.03
- counts: int32 [4, 128], P('group', 'curve'), may hold values from 64 to 128
- neighbours_first: int32 [4, 128, 6], P('group', 'curve'), may hold values from 0 to 23, as said below
- sends_first: int32 [4, 64], P('group', 'curve'), may hold values from 0 to 15, as said below
- new_slot: int32 [4, 128], P('group', 'curve'), may hold values from 0 to 63, as said below
- neighbours_second: int32 [4, 128, 6], P('group', 'curve'), may hold values from 0 to 23, as said below
- sends_second: int32 [4, 64], P('group', 'curve'), may hold values from 0 to 15, as said below
Outputs:
- positions_out: float32 [4, 128, 3, 128], P('group', 'curve')
- velocities_out: float32 [4, 128, 3, 128], P('group', 'curve')
- densities_out: float32 [4, 128, 128], P('group', 'curve')
The draws below stay inside these ranges and needn't reach their ends.
Inputs may be any that keep to these rules, and one draw needn't show every extreme that they name: `positions`: the particles of blocks c * 16 to c * 16 + 15 of every group have first component in [0.6 c, 0.6 c + 1) and other components in [0, 1). `neighbours_first`: A block's list holds 6 distinct candidate numbers, never the block's own slot. `neighbours_second`: A block's list holds 6 distinct candidate numbers, never the block's own slot. `sends_first`: each of a device's two lists of 4 holds distinct slots. `sends_second`: each of a device's two lists of 4 holds distinct slots. For each curve segment, new_slot over all groups' blocks of that segment is a permutation; from one device at most 2 blocks go to any one other group, and in every segment some device sends exactly 2 to some other group.
All inputs are finite; a program needn't handle non-finite values.
Results may differ from the reference program's by a relative error of at most 0.0003.
Values sent between devices are 32-bit elements; how exact they have to be, the bound alone decides.
A program may use at most 64 MiB of HBM per device.

```python
import math
import jax
import jax.numpy as jnp
from jax import lax

P_SIZE = 128
BLK_DEV = 16
NBR = 6
HALO = 4
MOVE_CAP = 2
NBLK = 128
N_CURVE = 8
N_GROUP = 4


def draw_positions(key, part):
    key_corner, key_inner = jax.random.split(jax.random.fold_in(key, 41))
    corner = 0.4 * jax.random.uniform(key_corner, (N_GROUP, NBLK, 3, 1), jnp.float32)
    inner = jax.random.uniform(key_inner, (N_GROUP, NBLK, 3, P_SIZE), jnp.float32)
    inner = 0.6 * jnp.minimum(inner, 0.999)
    segment = (jnp.arange(NBLK, dtype=jnp.int32) // BLK_DEV).astype(jnp.float32)
    first_axis = (jnp.arange(3, dtype=jnp.int32) == 0).astype(jnp.float32)
    base = 0.6 * segment[None, :, None, None] * first_axis[None, None, :, None]
    return (base + corner + inner).astype(jnp.float32)


def neighbour_draw(key):
    choices_all = BLK_DEV + 2 * HALO
    scores = jax.random.randint(key, (N_GROUP, NBLK, choices_all), 0, 1 << 20) * choices_all
    scores = scores + jnp.arange(choices_all, dtype=jnp.int32)[None, None, :]
    own = (jnp.arange(NBLK, dtype=jnp.int32) % BLK_DEV)[None, :, None] == jnp.arange(choices_all, dtype=jnp.int32)[None, None, :]
    scores = jnp.where(own, (1 << 20) * choices_all + choices_all, scores)
    order = jnp.argsort(scores, axis=-1)[..., :NBR]
    return order.astype(jnp.int32)


def send_draw(key):
    scores = jax.random.randint(key, (N_GROUP, N_CURVE, 2, BLK_DEV), 0, 1 << 20) * BLK_DEV
    scores = scores + jnp.arange(BLK_DEV, dtype=jnp.int32)
    order = jnp.argsort(scores, axis=-1)[..., :HALO]
    return order.reshape(N_GROUP, N_CURVE * 2 * HALO).astype(jnp.int32)


def draw_neighbours_first(key, part):
    return neighbour_draw(jax.random.fold_in(key, 11))


def draw_neighbours_second(key, part):
    return neighbour_draw(jax.random.fold_in(key, 12))


def draw_sends_first(key, part):
    return send_draw(jax.random.fold_in(key, 21))


def draw_sends_second(key, part):
    return send_draw(jax.random.fold_in(key, 22))


def segment_slots(key):
    key_one, key_two, key_three, key_four = jax.random.split(key, 4)
    members = jnp.arange(N_GROUP, dtype=jnp.int32)
    raw = jnp.maximum(jax.random.randint(key_one, (N_GROUP, N_GROUP), 0, 5) - 2, 0)
    upper = jnp.triu(raw, 1)
    amounts = upper + upper.T
    first = jax.random.randint(key_two, (), 0, N_GROUP)
    second = (first + 1 + jax.random.randint(key_three, (), 0, N_GROUP - 1)) % N_GROUP
    forced = (members[:, None] == first) & (members[None, :] == second) | (members[:, None] == second) & (members[None, :] == first)
    amounts = jnp.where(forced, MOVE_CAP, amounts)
    offsets = jnp.cumsum(amounts, axis=1) - amounts
    perms = jax.vmap(lambda inner: jax.random.permutation(inner, BLK_DEV))(jax.random.split(key_four, N_GROUP)).astype(jnp.int32)
    ranks = jnp.arange(BLK_DEV, dtype=jnp.int32)
    inside = (ranks[None, None, :] >= offsets[:, :, None]) & (ranks[None, None, :] < (offsets + amounts)[:, :, None])
    partner = jnp.sum(inside.astype(jnp.int32) * members[None, :, None], axis=1)
    moving = jnp.sum(inside.astype(jnp.int32), axis=1) > 0
    within = ranks[None, :] - jnp.take_along_axis(offsets, partner, axis=1)
    partner_rank = jnp.clip(offsets[partner, members[:, None]] + within, 0, BLK_DEV - 1)
    partner_slot = perms[partner, partner_rank]
    at_rank = jnp.where(moving, partner * BLK_DEV + partner_slot, members[:, None] * BLK_DEV + perms)
    inverse = jnp.argsort(perms, axis=1)
    return jnp.take_along_axis(at_rank, inverse, axis=1)


def draw_new_slot(key, part):
    keys = jax.random.split(jax.random.fold_in(key, 31), N_CURVE)
    table = jax.vmap(segment_slots)(keys)
    return jnp.transpose(table, (1, 0, 2)).reshape(N_GROUP, NBLK).astype(jnp.int32)


def place_ends(array, own_key, least, largest):
    place = [jax.random.randint(jax.random.fold_in(own_key, axis), (), 0, length) for axis, length in enumerate(array.shape)]
    widest = array.shape.index(max(array.shape))
    neighbour = place[:widest] + [(place[widest] + 1) % array.shape[widest]] + place[widest + 1:]
    return array.at[tuple(place)].set(least).at[tuple(neighbour)].set(largest)


def block_scale(own_key, extent, shards, smallest, largest):
    factor_of = 1.0
    for dim, shards_of in shards:
        steps = jax.random.uniform(jax.random.fold_in(jax.random.fold_in(own_key, 6), dim), (shards_of,), jnp.float32, smallest / len(shards), largest / len(shards))
        factor_of = factor_of * jnp.repeat(jnp.exp(steps), extent[dim] // shards_of).reshape((-1,) + (1,) * (len(extent) - 1 - dim))
    return factor_of


def bell_draw(stream_key, extent, deviation, most, pieces=(), kind=jnp.bfloat16):
    drawn = jax.random.normal(stream_key, extent, jnp.float32) * deviation
    if len(pieces) > 0:
        drawn = block_scale(stream_key, extent, pieces, -0.22, 0.18) * drawn
    return jnp.clip(drawn, min=-most, max=most).astype(kind)


def setup_inputs(seed: int = 0) -> dict:
    streams_of = jax.random.split(jax.random.key(seed), 10)
    return {
        "positions": draw_positions(jax.random.fold_in(streams_of[9], 71), 0),
        "velocities": bell_draw(streams_of[1], (N_GROUP, NBLK, 3, P_SIZE), 0.5, 3.0, ((0, 4), (1, 8)), jnp.float32),
        "masses": jnp.clip(jnp.exp(math.log(0.03) - 2.3025851 * jax.random.uniform(streams_of[2], (N_GROUP, NBLK, P_SIZE), jnp.float32) ** block_scale(streams_of[2], (N_GROUP, NBLK, P_SIZE), ((0, 4), (1, 8)), -0.2, 0.2)), 0.003, 0.03),
        "counts": place_ends(jax.random.randint(streams_of[3], (N_GROUP, NBLK), P_SIZE // 2, P_SIZE + 1), jax.random.fold_in(streams_of[3], 1), P_SIZE // 2, P_SIZE).astype(jnp.int32),
        "neighbours_first": draw_neighbours_first(jax.random.fold_in(streams_of[9], 71), 0),
        "sends_first": draw_sends_first(jax.random.fold_in(streams_of[9], 71), 0),
        "new_slot": draw_new_slot(jax.random.fold_in(streams_of[9], 71), 0),
        "neighbours_second": draw_neighbours_second(jax.random.fold_in(streams_of[9], 71), 0),
        "sends_second": draw_sends_second(jax.random.fold_in(streams_of[9], 71), 0),
    }


KERNEL_SCALE = 4.0
SMOOTHING = 0.5
SOFTENING = 0.0025
BACKGROUND = 0.5
TIME_STEP = 0.1


def kernel_density(target_x, source_x, source_mass):
    offsets = [target_x[:, None, axis_id, :, None] - source_x[:, :, axis_id, None, :] for axis_id in range(3)]
    square = offsets[0] * offsets[0] + offsets[1] * offsets[1] + offsets[2] * offsets[2]
    weight = jnp.exp(-KERNEL_SCALE * square)
    return BACKGROUND + jnp.sum(weight * source_mass[:, :, None, :], axis=(1, 3))


def kernel_force(target_x, target_v, target_rho, source_x, source_v, source_mass, source_rho):
    offsets = [target_x[:, None, axis_id, :, None] - source_x[:, :, axis_id, None, :] for axis_id in range(3)]
    square = offsets[0] * offsets[0] + offsets[1] * offsets[1] + offsets[2] * offsets[2]
    approach = offsets[0] * (target_v[:, None, 0, :, None] - source_v[:, :, 0, None, :])
    approach = approach + offsets[1] * (target_v[:, None, 1, :, None] - source_v[:, :, 1, None, :])
    approach = approach + offsets[2] * (target_v[:, None, 2, :, None] - source_v[:, :, 2, None, :])
    weight = jnp.exp(-KERNEL_SCALE * square)
    closing = SMOOTHING * jnp.minimum(approach, 0.0) / (square + SOFTENING)
    mine = target_rho[:, None, :, None]
    theirs = source_rho[:, :, None, :]
    factor = source_mass[:, :, None, :] * (1.0 / mine + 1.0 / theirs - closing / (0.5 * (mine + theirs)))
    factor = factor * (2.0 * KERNEL_SCALE) * weight
    return jnp.stack([jnp.sum(factor * offsets[axis_id], axis=(1, 3)) for axis_id in range(3)], axis=1)


def batched(function, arrays):
    shaped = tuple(item.reshape((item.shape[0] // 4, 4) + item.shape[1:]) for item in arrays)
    result = lax.map(lambda piece: function(*piece), shaped)
    return result.reshape((-1,) + result.shape[2:])


def candidate_table(field, sends):
    outgoing = jax.vmap(lambda blocks, picks: jnp.take(blocks, picks, axis=0))(field, sends)
    half = sends.shape[1] // 2
    lower = jnp.roll(outgoing, 1, axis=0)[:, half:]
    upper = jnp.roll(outgoing, -1, axis=0)[:, :half]
    return jnp.concatenate([field, lower, upper], axis=1)


def group_step(positions, velocities, mass_live, neighbours, sends):
    segments = positions.shape[0] // BLK_DEV
    shape_of = lambda item: item.reshape((segments, BLK_DEV) + item.shape[1:])
    picks = sends.reshape(segments, -1)
    own = jnp.broadcast_to(jnp.arange(BLK_DEV, dtype=jnp.int32)[None, :, None], (segments, BLK_DEV, 1))
    index = jnp.concatenate([own, shape_of(neighbours).astype(jnp.int32)], axis=2)

    def pick(field):
        table = candidate_table(shape_of(field), picks)
        chosen = jax.vmap(lambda block_table, rows: jnp.take(block_table, rows, axis=0))(table, index)
        return chosen.reshape((segments * BLK_DEV,) + chosen.shape[2:])

    source_x = pick(positions)
    source_m = pick(mass_live)
    density = batched(kernel_density, (positions, source_x, source_m))
    accel = batched(kernel_force, (positions, velocities, density, source_x, pick(velocities), source_m, pick(density)))
    new_velocity = velocities + TIME_STEP * accel
    new_position = positions + TIME_STEP * new_velocity
    return new_position, new_velocity, density


def migrate(field, new_slot):
    groups, blocks = field.shape[0], field.shape[1]
    segments = blocks // BLK_DEV
    rest = field.shape[2:]
    moved = field.reshape((groups, segments, BLK_DEV) + rest)
    moved = jnp.moveaxis(moved, 0, 1).reshape((segments, groups * BLK_DEV) + rest)
    target = jnp.moveaxis(new_slot.reshape(groups, segments, BLK_DEV), 0, 1).reshape(segments, groups * BLK_DEV)
    rows = jnp.arange(segments, dtype=jnp.int32)[:, None]
    placed = jnp.zeros_like(moved).at[rows, target.astype(jnp.int32)].set(moved)
    placed = placed.reshape((segments, groups, BLK_DEV) + rest)
    return jnp.moveaxis(placed, 1, 0).reshape(field.shape)


def reference(positions, velocities, masses, counts, neighbours_first, sends_first, new_slot, neighbours_second, sends_second):
    slots = jnp.arange(masses.shape[-1], dtype=jnp.int32)
    live = (slots[None, None, :] < counts[:, :, None]).astype(masses.dtype)
    mass_live = masses * live
    first_x, first_v, first_rho = lax.map(lambda item: group_step(*item), (positions, velocities, mass_live, neighbours_first, sends_first))
    moved_x = migrate(first_x, new_slot)
    moved_v = migrate(first_v, new_slot)
    moved_m = migrate(mass_live, new_slot)
    final_x, final_v, final_rho = lax.map(lambda item: group_step(*item), (moved_x, moved_v, moved_m, neighbours_second, sends_second))
    return final_x, final_v, final_rho
```

```python
import functools
import math

import jax
import jax.numpy as jnp
from jax import lax
from jax.experimental import pallas as pl
from jax.experimental.pallas import tpu as pltpu
from jax.sharding import PartitionSpec as P

KERNEL_SCALE = 4.0
SOFTENING = 0.0025
BACKGROUND = 0.5
TIME_STEP = 0.1
SPACING = 0.6
MOVE_CAP = 2
LOG2E = math.log2(math.e)
SCALE = -KERNEL_SCALE * LOG2E
DEAD = -200.0
MESH = pl.DeviceIdType.MESH
F32 = jnp.float32
BF16 = jnp.bfloat16


def split(value):
    high = value.astype(BF16).astype(F32)
    rest = value - high
    middle = rest.astype(BF16).astype(F32)
    return high, middle, rest - middle


def source_rows(value):
    high, middle, low = split(value)
    return [high, middle, low, high, high, middle]


def target_rows(value):
    high, middle, low = split(value)
    return [high, high, high, middle, low, middle]


def rows_of(shape):
    return lax.broadcasted_iota(jnp.int32, shape, 0)


def moments(state, corner):
    row = rows_of(state.shape)
    state = state - jnp.where(row == 0, corner + 0.5, jnp.where(row < 3, 0.5, 0.0))
    square = jnp.sum(jnp.where(row < 3, state * state, 0.0), axis=0, keepdims=True)
    after = pltpu.roll(state, 3, 0)
    cross = jnp.sum(
        jnp.where((row >= 3) & (row < 6), state * after, 0.0), axis=0, keepdims=True
    )
    return row, state, after, square, cross


def prepare_source(state, corner, source_t, source_m):
    row, state, after, square, cross = moments(state, corner)
    mass = state[6:7]
    logm = jnp.where(mass > 0.0, jnp.log(jnp.maximum(mass, 1e-30)) * LOG2E, DEAD)
    lower = jnp.where(row < 6, state, jnp.where(row == 6, 1.0, square))
    upper = jnp.where(row == 0, cross, jnp.where(row == 1, logm, 0.0))
    feature = jnp.concatenate([lower, upper], axis=0)
    width = state.shape[1]
    pieces = source_rows(feature)
    used = len(pieces) * feature.shape[0]
    pieces.append(jnp.zeros((width - used, width), F32))
    source_t[...] = jnp.concatenate(pieces, axis=0).T.astype(BF16)
    weighted = jnp.where(row < 7, lower * mass, 0.0)
    source_m[...] = jnp.concatenate(
        list(split(weighted)) + [jnp.zeros_like(weighted)], axis=0
    ).astype(BF16)


def prepare_target(state, corner, target_d, target_f):
    row, state, after, square, cross = moments(state, corner)
    width = state.shape[1]
    ahead = pltpu.roll(state, state.shape[0] - 3, 0)
    near = jnp.where(row < 3, (-2.0 * SCALE) * state, 0.0)
    tail = jnp.where(row == 7, SCALE, 0.0)
    plain = jnp.where(row == 6, SCALE * square, near + tail)
    soft = jnp.where(row == 6, SCALE * (square + SOFTENING), near + tail)
    closing = jnp.where(
        row < 3,
        -SCALE * ahead,
        jnp.where(row < 6, -SCALE * after, jnp.where(row == 6, SCALE * cross, 0.0)),
    )
    upper_d = jnp.where(row == 1, 1.0, 0.0)
    upper_c = jnp.where(row == 0, SCALE, 0.0)

    def table(lower, upper):
        pieces = target_rows(jnp.concatenate([lower, upper], axis=0))
        used = len(pieces) * 2 * lower.shape[0]
        pieces.append(jnp.zeros((width - used, width), F32))
        return jnp.concatenate(pieces, axis=0).astype(BF16)

    target_d[...] = table(plain, upper_d)
    target_f[:, 0:width] = table(soft, jnp.zeros_like(upper_c))
    target_f[:, width : 2 * width] = table(closing, upper_c)


def density_of(block, nbr, source_t, target_d):
    count = nbr.shape[0]
    target = target_d[block]
    total = None
    for item in range(count + 1):
        pick = block if item == 0 else nbr[item - 1, 0, block]
        power = jnp.dot(source_t[pick], target, preferred_element_type=F32)
        weight = jnp.exp2(power)
        total = weight if total is None else total + weight
    return BACKGROUND + jnp.sum(total, axis=0, keepdims=True)


def force_of(block, nbr, state, corner, rho, rho_col, inv_col, source_t, source_m, target_f):
    count = nbr.shape[0]
    width = state.shape[1]
    target = target_f[block]
    inverse = 1.0 / rho
    total = None
    for item in range(count + 1):
        pick = block if item == 0 else nbr[item - 1, 0, block]
        both = jnp.dot(source_t[pick], target, preferred_element_type=F32)
        soft = both[:, 0:width]
        closing = jnp.maximum(both[:, width : 2 * width], 0.0)
        bottom = soft * (rho_col[pick] + rho)
        viscous = closing * pl.reciprocal(bottom, approx=True)
        factor = jnp.exp2(soft) * (inv_col[pick] + inverse - viscous)
        part = jnp.dot(source_m[pick], factor.astype(BF16), preferred_element_type=F32)
        total = part if total is None else total + part
    rows = state.shape[0]
    sums = total[0:rows] + total[rows : 2 * rows] + total[2 * rows : 3 * rows]
    row = rows_of(state.shape)
    centred = state - jnp.where(row == 0, corner + 0.5, jnp.where(row < 3, 0.5, 0.0))
    strength = 2.0 * KERNEL_SCALE * math.exp(KERNEL_SCALE * SOFTENING)
    accel = strength * (centred * sums[6:7] - sums)
    velocity = state + TIME_STEP * pltpu.roll(accel, 3, 0)
    position = state + TIME_STEP * pltpu.roll(velocity, rows - 3, 0)
    return jnp.where(row < 3, position, jnp.where(row < 6, velocity, state))


def columns(rho, rho_col, inv_col):
    width = rho.shape[1]
    col = jnp.broadcast_to(rho, (width, width)).T
    rho_col[...] = col
    inv_col[...] = 1.0 / col


def kernel(
    n_curve, n_group,
    pos, vel, mass, counts, nbr1, sends1, slots_s, slots_v, nbr2, sends2,
    pos_out, vel_out, rho_out,
    table1, table2, land1, land2, kept, moved, out1, out2, out_m, rho1, rho2, rho_s1, rho_s2,
    source_t, source_m, target_d, target_f, rho_col, inv_col,
    slots_own, slots_in, code_v, code_s,
    send_sem, recv_sem, send_g, recv_g, code_sem,
):
    blocks = pos.shape[2]
    width = pos.shape[3]
    halo = sends1.shape[1] // 2
    mine = lax.axis_index("curve")
    group = lax.axis_index("group")
    lower = lax.rem(mine + n_curve - 1, n_curve)
    upper = lax.rem(mine + 1, n_curve)
    corner = SPACING * mine.astype(F32)
    barrier = pltpu.get_barrier_semaphore()
    for other in (lower, upper):
        pl.semaphore_signal(barrier, inc=1, device_id={"curve": other}, device_id_type=MESH)
    peers = [lax.rem(group + step, n_group) for step in range(1, n_group)]
    for other in peers:
        pl.semaphore_signal(barrier, inc=1, device_id={"group": other}, device_id_type=MESH)

    lane = lax.broadcasted_iota(jnp.int32, (1, width), 1)

    def load_state(block, carry):
        for axis in range(3):
            table1[block, axis : axis + 1, :] = pos[0, axis, pl.ds(block, 1), :]
            table1[block, 3 + axis : 4 + axis, :] = vel[0, axis, pl.ds(block, 1), :]
        live = jnp.where(lane < counts[0, block], mass[0, pl.ds(block, 1), :], 0.0)
        table1[block, 6:7, :] = live
        table1[block, 7:8, :] = jnp.zeros_like(live)
        return carry

    lax.fori_loop(0, blocks, load_state, 0, unroll=True)
    slots_own[...] = jnp.full(slots_own.shape, -1, jnp.int32)
    slots_own[:, 0:blocks] = slots_v[...]
    for item in range(2 * halo):
        out1[item] = table1[sends1[0, item]]
    pl.semaphore_wait(barrier, 2 + n_group - 1)

    def exchange(outgoing, landing, start, base):
        copies = []
        for side, other in ((0, lower), (1, upper)):
            copies.append(
                pltpu.make_async_remote_copy(
                    src_ref=outgoing.at[pl.ds(side * halo, halo)],
                    dst_ref=landing.at[pl.ds(start + (1 - side) * halo, halo)],
                    send_sem=send_sem.at[base + side],
                    recv_sem=recv_sem.at[base + side],
                    device_id={"curve": other},
                    device_id_type=MESH,
                )
            )
        for copy in copies:
            copy.start()
        return copies

    def finish(copies):
        for copy in copies:
            copy.wait()

    first = exchange(out1, land1, 0, 0)
    lists = []
    for step, other in enumerate(peers):
        copy = pltpu.make_async_remote_copy(
            src_ref=slots_own,
            dst_ref=slots_in.at[step],
            send_sem=send_g.at[step],
            recv_sem=recv_g.at[step],
            device_id={"group": other},
            device_id_type=MESH,
        )
        copy.start()
        lists.append(copy)

    def prepare_own(table):
        def run(block, carry):
            state = table[block]
            prepare_source(state, corner, source_t.at[block], source_m.at[block])
            prepare_target(state, corner, target_d.at[block], target_f.at[block])
            return carry

        lax.fori_loop(0, blocks, run, 0)

    def prepare_halo(land):
        def run(item, carry):
            block = blocks + item
            prepare_source(land[item], corner, source_t.at[block], source_m.at[block])
            return carry

        lax.fori_loop(0, 2 * halo, run, 0)

    def sph(table, land, nbr, sends, rho, rho_send, base, write):
        prepare_halo(land)

        def listed(item, carry):
            rho_send[item] = density_of(sends[0, item], nbr, source_t, target_d)
            return carry

        lax.fori_loop(0, 2 * halo, listed, 0)
        copies = exchange(rho_send, rho, blocks, base)

        def own(block, carry):
            value = density_of(block, nbr, source_t, target_d)
            rho[block] = value
            columns(value, rho_col.at[block], inv_col.at[block])
            return carry

        lax.fori_loop(0, blocks, own, 0)
        finish(copies)

        def halos(block, carry):
            columns(rho[block], rho_col.at[block], inv_col.at[block])
            return carry

        lax.fori_loop(blocks, blocks + 2 * halo, halos, 0)

        def push(block, carry):
            write(
                block,
                force_of(
                    block, nbr, table[block], corner, rho[block],
                    rho_col, inv_col, source_t, source_m, target_f,
                ),
            )
            return carry

        lax.fori_loop(0, blocks, push, 0)

    prepare_own(table1)
    finish(lists)
    wanted = rows_of((blocks, width)) + group * blocks
    lanes = lax.broadcasted_iota(jnp.int32, (blocks, width), 1)
    code = jnp.sum(jnp.where(slots_own[...] == wanted, lanes, 0), axis=1, keepdims=True)
    for step in range(n_group - 1):
        arrived = slots_in[step]
        here = (arrived >= group * blocks) & (arrived < (group + 1) * blocks)
        lead = jnp.min(jnp.where(here, lane, width), axis=1, keepdims=True)
        place = blocks + MOVE_CAP * step + jnp.where(lane > lead, 1, 0)
        code = code + jnp.sum(jnp.where(arrived == wanted, place, 0), axis=1, keepdims=True)
    code = jnp.minimum(code, moved.shape[0] - 1)
    code_v[...] = jnp.broadcast_to(code, code_v.shape)
    code_copy = pltpu.make_async_copy(code_v, code_s, code_sem)
    code_copy.start()
    finish(first)

    def keep(block, state):
        kept[block] = state

    sph(table1, land1, nbr1, sends1, rho1, rho_s1, 2, keep)

    moves = []
    for step, other in enumerate(peers):
        one = jnp.int32(0)
        two = jnp.int32(0)
        for block in reversed(range(blocks)):
            target = slots_s[0, block]
            goes = (target >= other * blocks) & (target < (other + 1) * blocks)
            two = jnp.where(goes, one, two)
            one = jnp.where(goes, block, one)
        out_m[step, 0] = kept[one]
        out_m[step, 1] = kept[two]
        copy = pltpu.make_async_remote_copy(
            src_ref=out_m.at[step],
            dst_ref=moved.at[pl.ds(blocks + MOVE_CAP * step, MOVE_CAP)],
            send_sem=send_g.at[n_group - 1 + step],
            recv_sem=recv_g.at[n_group - 1 + step],
            device_id={"group": other},
            device_id_type=MESH,
        )
        copy.start()
        moves.append(copy)
    code_copy.wait()
    for block in range(blocks):
        moved[block] = kept[block]
    finish(moves)
    for item in range(2 * halo):
        out2[item] = moved[code_s[sends2[0, item], 0]]
    second = exchange(out2, land2, 0, 4)
    for block in range(blocks):
        table2[block] = moved[code_s[block, 0]]
    prepare_own(table2)
    finish(second)

    def emit(block, state):
        for axis in range(3):
            pos_out[0, axis, pl.ds(block, 1), :] = state[axis : axis + 1]
            vel_out[0, axis, pl.ds(block, 1), :] = state[3 + axis : 4 + axis]
        rho_out[0, pl.ds(block, 1), :] = rho2[block]

    sph(table2, land2, nbr2, sends2, rho2, rho_s2, 6, emit)


def body(
    n_curve, n_group,
    positions, velocities, masses, counts, neighbours_first, sends_first, new_slot,
    neighbours_second, sends_second,
):
    blocks, width = masses.shape[1], masses.shape[2]
    halo = sends_first.shape[1] // 2
    whole = blocks + 2 * halo
    peers = n_group - 1
    vmem = pl.BlockSpec(memory_space=pltpu.VMEM)
    smem = pl.BlockSpec(memory_space=pltpu.SMEM)
    scratch = [
        pltpu.VMEM((blocks, 8, width), F32),
        pltpu.VMEM((blocks, 8, width), F32),
        pltpu.VMEM((2 * halo, 8, width), F32),
        pltpu.VMEM((2 * halo, 8, width), F32),
        pltpu.VMEM((blocks, 8, width), F32),
        pltpu.VMEM((blocks + MOVE_CAP * peers, 8, width), F32),
        pltpu.VMEM((2 * halo, 8, width), F32),
        pltpu.VMEM((2 * halo, 8, width), F32),
        pltpu.VMEM((peers, MOVE_CAP, 8, width), F32),
        pltpu.VMEM((whole, 1, width), F32),
        pltpu.VMEM((whole, 1, width), F32),
        pltpu.VMEM((2 * halo, 1, width), F32),
        pltpu.VMEM((2 * halo, 1, width), F32),
        pltpu.VMEM((whole, width, width), BF16),
        pltpu.VMEM((whole, 32, width), BF16),
        pltpu.VMEM((blocks, width, width), BF16),
        pltpu.VMEM((blocks, width, 2 * width), BF16),
        pltpu.VMEM((whole, width, width), F32),
        pltpu.VMEM((whole, width, width), F32),
        pltpu.VMEM((1, width), jnp.int32),
        pltpu.VMEM((peers, 1, width), jnp.int32),
        pltpu.VMEM((blocks, width), jnp.int32),
        pltpu.SMEM((blocks, width), jnp.int32),
        pltpu.SemaphoreType.DMA((8,)),
        pltpu.SemaphoreType.DMA((8,)),
        pltpu.SemaphoreType.DMA((2 * peers,)),
        pltpu.SemaphoreType.DMA((2 * peers,)),
        pltpu.SemaphoreType.DMA,
    ]
    turned = jax.ShapeDtypeStruct((1, 3, blocks, width), F32)
    positions_out, velocities_out, densities_out = pl.pallas_call(
        functools.partial(kernel, n_curve, n_group),
        out_shape=(
            turned,
            turned,
            jax.ShapeDtypeStruct(masses.shape, F32),
        ),
        in_specs=[vmem, vmem, vmem, smem, smem, smem, smem, vmem, smem, smem],
        out_specs=(vmem, vmem, vmem),
        scratch_shapes=scratch,
        compiler_params=pltpu.CompilerParams(
            collective_id=0, has_side_effects=True, vmem_limit_bytes=32 * 1024 * 1024
        ),
        name="sph",
    )(
        positions.transpose(0, 2, 1, 3), velocities.transpose(0, 2, 1, 3), masses, counts,
        neighbours_first.transpose(2, 0, 1), sends_first, new_slot,
        new_slot, neighbours_second.transpose(2, 0, 1), sends_second,
    )
    return (
        positions_out.transpose(0, 2, 1, 3), velocities_out.transpose(0, 2, 1, 3), densities_out,
    )


def solution(mesh):
    blocks4 = P("group", "curve", None, None)
    blocks3 = P("group", "curve", None)
    blocks2 = P("group", "curve")
    in_specs = (
        blocks4, blocks4, blocks3, blocks2, blocks3, blocks2, blocks2, blocks3, blocks2,
    )
    return jax.shard_map(
        functools.partial(body, mesh.shape["curve"], mesh.shape["group"]),
        mesh=mesh, in_specs=in_specs, out_specs=(blocks4, blocks4, blocks3), check_vma=False,
    )
```

```python
import functools
import math

import jax
import jax.numpy as jnp
from jax import lax
from jax.experimental import pallas as pl
from jax.experimental.pallas import tpu as pltpu
from jax.sharding import PartitionSpec as P

KERNEL_SCALE = 4.0
SOFTENING = 0.0025
BACKGROUND = 0.5
TIME_STEP = 0.1
SPACING = 0.6
MOVE_CAP = 2
LOG2E = math.log2(math.e)
SCALE = -KERNEL_SCALE * LOG2E
DEAD = -200.0
MESH = pl.DeviceIdType.MESH
F32 = jnp.float32
BF16 = jnp.bfloat16


def split(value):
    high = value.astype(BF16).astype(F32)
    rest = value - high
    middle = rest.astype(BF16).astype(F32)
    return high, middle, rest - middle


def source_rows(value):
    high, middle, low = split(value)
    return [high, middle, low, high, high, middle]


def target_rows(value):
    high, middle, low = split(value)
    return [high, high, high, middle, low, middle]


def rows_of(shape):
    return lax.broadcasted_iota(jnp.int32, shape, 0)


def moments(state, corner):
    row = rows_of(state.shape)
    state = state - jnp.where(row == 0, corner + 0.5, jnp.where(row < 3, 0.5, 0.0))
    square = jnp.sum(jnp.where(row < 3, state * state, 0.0), axis=0, keepdims=True)
    after = pltpu.roll(state, 3, 0)
    cross = jnp.sum(
        jnp.where((row >= 3) & (row < 6), state * after, 0.0), axis=0, keepdims=True
    )
    return row, state, after, square, cross


def prepare_source(state, corner, source_t, source_m):
    row, state, after, square, cross = moments(state, corner)
    mass = state[6:7]
    logm = jnp.where(mass > 0.0, jnp.log(jnp.maximum(mass, 1e-30)) * LOG2E, DEAD)
    lower = jnp.where(row < 6, state, jnp.where(row == 6, 1.0, square))
    upper = jnp.where(row == 0, cross, jnp.where(row == 1, logm, 0.0))
    feature = jnp.concatenate([lower, upper], axis=0)
    width = state.shape[1]
    pieces = source_rows(feature)
    used = len(pieces) * feature.shape[0]
    pieces.append(jnp.zeros((width - used, width), F32))
    source_t[...] = jnp.concatenate(pieces, axis=0).T.astype(BF16)
    weighted = jnp.where(row < 7, lower * mass, 0.0)
    source_m[...] = jnp.concatenate(
        list(split(weighted)) + [jnp.zeros_like(weighted)], axis=0
    ).astype(BF16)


def prepare_target(state, corner, target_d, target_f):
    row, state, after, square, cross = moments(state, corner)
    width = state.shape[1]
    ahead = pltpu.roll(state, state.shape[0] - 3, 0)
    near = jnp.where(row < 3, (-2.0 * SCALE) * state, 0.0)
    tail = jnp.where(row == 7, SCALE, 0.0)
    plain = jnp.where(row == 6, SCALE * square, near + tail)
    soft = jnp.where(row == 6, SCALE * (square + SOFTENING), near + tail)
    closing = jnp.where(
        row < 3,
        -SCALE * ahead,
        jnp.where(row < 6, -SCALE * after, jnp.where(row == 6, SCALE * cross, 0.0)),
    )
    upper_d = jnp.where(row == 1, 1.0, 0.0)
    upper_c = jnp.where(row == 0, SCALE, 0.0)

    def table(lower, upper):
        pieces = target_rows(jnp.concatenate([lower, upper], axis=0))
        used = len(pieces) * 2 * lower.shape[0]
        pieces.append(jnp.zeros((width - used, width), F32))
        return jnp.concatenate(pieces, axis=0).astype(BF16)

    target_d[...] = table(plain, upper_d)
    target_f[:, 0:width] = table(soft, jnp.zeros_like(upper_c))
    target_f[:, width : 2 * width] = table(closing, upper_c)


def density_of(block, nbr, source_t, target_d):
    count = nbr.shape[0]
    target = target_d[block]
    total = None
    for item in range(count + 1):
        pick = block if item == 0 else nbr[item - 1, 0, block]
        power = jnp.dot(source_t[pick], target, preferred_element_type=F32)
        weight = jnp.exp2(power)
        total = weight if total is None else total + weight
    return BACKGROUND + jnp.sum(total, axis=0, keepdims=True)


def force_of(block, nbr, state, corner, rho, rho_col, inv_col, source_t, source_m, target_f):
    count = nbr.shape[0]
    width = state.shape[1]
    target = target_f[block]
    inverse = 1.0 / rho
    total = None
    for item in range(count + 1):
        pick = block if item == 0 else nbr[item - 1, 0, block]
        both = jnp.dot(source_t[pick], target, preferred_element_type=F32)
        soft = both[:, 0:width]
        closing = jnp.maximum(both[:, width : 2 * width], 0.0)
        bottom = soft * (rho_col[pick] + rho)
        viscous = closing * pl.reciprocal(bottom, approx=True)
        factor = jnp.exp2(soft) * (inv_col[pick] + inverse - viscous)
        part = jnp.dot(source_m[pick], factor.astype(BF16), preferred_element_type=F32)
        total = part if total is None else total + part
    rows = state.shape[0]
    sums = total[0:rows] + total[rows : 2 * rows] + total[2 * rows : 3 * rows]
    row = rows_of(state.shape)
    centred = state - jnp.where(row == 0, corner + 0.5, jnp.where(row < 3, 0.5, 0.0))
    strength = 2.0 * KERNEL_SCALE * math.exp(KERNEL_SCALE * SOFTENING)
    accel = strength * (centred * sums[6:7] - sums)
    velocity = state + TIME_STEP * pltpu.roll(accel, 3, 0)
    position = state + TIME_STEP * pltpu.roll(velocity, rows - 3, 0)
    return jnp.where(row < 3, position, jnp.where(row < 6, velocity, state))


def columns(rho, rho_col, inv_col):
    width = rho.shape[1]
    col = jnp.broadcast_to(rho, (width, width)).T
    rho_col[...] = col
    inv_col[...] = 1.0 / col


def kernel(
    n_curve, n_group,
    pos, vel, mass, counts, nbr1, sends1, slots_s, slots_v, nbr2, sends2,
    pos_out, vel_out, rho_out,
    table1, table2, land1, land2, kept, moved, out1, out2, out_m, rho1, rho2, rho_s1, rho_s2,
    source_t, source_m, target_d, target_f, rho_col, inv_col,
    slots_own, slots_in, code_v, code_s,
    send_sem, recv_sem, send_g, recv_g, code_sem,
):
    blocks = pos.shape[2]
    width = pos.shape[3]
    halo = sends1.shape[1] // 2
    mine = lax.axis_index("curve")
    group = lax.axis_index("group")
    lower = lax.rem(mine + n_curve - 1, n_curve)
    upper = lax.rem(mine + 1, n_curve)
    corner = SPACING * mine.astype(F32)
    barrier = pltpu.get_barrier_semaphore()
    for other in (lower, upper):
        pl.semaphore_signal(barrier, inc=1, device_id={"curve": other}, device_id_type=MESH)
    peers = [lax.rem(group + step, n_group) for step in range(1, n_group)]
    for other in peers:
        pl.semaphore_signal(barrier, inc=1, device_id={"group": other}, device_id_type=MESH)

    lane = lax.broadcasted_iota(jnp.int32, (1, width), 1)

    def load_state(block, carry):
        for axis in range(3):
            table1[block, axis : axis + 1, :] = pos[0, axis, pl.ds(block, 1), :]
            table1[block, 3 + axis : 4 + axis, :] = vel[0, axis, pl.ds(block, 1), :]
        live = jnp.where(lane < counts[0, block], mass[0, pl.ds(block, 1), :], 0.0)
        table1[block, 6:7, :] = live
        table1[block, 7:8, :] = jnp.zeros_like(live)
        return carry

    lax.fori_loop(0, blocks, load_state, 0, unroll=True)
    slots_own[...] = jnp.full(slots_own.shape, -1, jnp.int32)
    slots_own[:, 0:blocks] = slots_v[...]
    for item in range(2 * halo):
        out1[item] = table1[sends1[0, item]]
    pl.semaphore_wait(barrier, 2 + n_group - 1)

    def exchange(outgoing, landing, start, base):
        copies = []
        for side, other in ((0, lower), (1, upper)):
            copies.append(
                pltpu.make_async_remote_copy(
                    src_ref=outgoing.at[pl.ds(side * halo, halo)],
                    dst_ref=landing.at[pl.ds(start + (1 - side) * halo, halo)],
                    send_sem=send_sem.at[base + side],
                    recv_sem=recv_sem.at[base + side],
                    device_id={"curve": other},
                    device_id_type=MESH,
                )
            )
        for copy in copies:
            copy.start()
        return copies

    def finish(copies):
        for copy in copies:
            copy.wait()

    first = exchange(out1, land1, 0, 0)
    lists = []
    for step, other in enumerate(peers):
        copy = pltpu.make_async_remote_copy(
            src_ref=slots_own,
            dst_ref=slots_in.at[step],
            send_sem=send_g.at[step],
            recv_sem=recv_g.at[step],
            device_id={"group": other},
            device_id_type=MESH,
        )
        copy.start()
        lists.append(copy)

    def prepare_own(table):
        def run(block, carry):
            state = table[block]
            prepare_source(state, corner, source_t.at[block], source_m.at[block])
            prepare_target(state, corner, target_d.at[block], target_f.at[block])
            return carry

        lax.fori_loop(0, blocks, run, 0, unroll=8)

    def prepare_halo(land):
        def run(item, carry):
            block = blocks + item
            prepare_source(land[item], corner, source_t.at[block], source_m.at[block])
            return carry

        lax.fori_loop(0, 2 * halo, run, 0, unroll=8)

    def sph(table, land, nbr, sends, rho, rho_send, base, write):
        prepare_halo(land)

        def listed(item, carry):
            rho_send[item] = density_of(sends[0, item], nbr, source_t, target_d)
            return carry

        lax.fori_loop(0, 2 * halo, listed, 0, unroll=4)
        copies = exchange(rho_send, rho, blocks, base)

        def own(block, carry):
            value = density_of(block, nbr, source_t, target_d)
            rho[block] = value
            columns(value, rho_col.at[block], inv_col.at[block])
            return carry

        lax.fori_loop(0, blocks, own, 0, unroll=4)
        finish(copies)

        def halos(block, carry):
            columns(rho[block], rho_col.at[block], inv_col.at[block])
            return carry

        lax.fori_loop(blocks, blocks + 2 * halo, halos, 0, unroll=8)

        def push(block, carry):
            write(
                block,
                force_of(
                    block, nbr, table[block], corner, rho[block],
                    rho_col, inv_col, source_t, source_m, target_f,
                ),
            )
            return carry

        lax.fori_loop(0, blocks, push, 0, unroll=4)

    prepare_own(table1)
    finish(lists)
    wanted = rows_of((blocks, width)) + group * blocks
    lanes = lax.broadcasted_iota(jnp.int32, (blocks, width), 1)
    code = jnp.sum(jnp.where(slots_own[...] == wanted, lanes, 0), axis=1, keepdims=True)
    for step in range(n_group - 1):
        arrived = slots_in[step]
        here = (arrived >= group * blocks) & (arrived < (group + 1) * blocks)
        lead = jnp.min(jnp.where(here, lane, width), axis=1, keepdims=True)
        place = blocks + MOVE_CAP * step + jnp.where(lane > lead, 1, 0)
        code = code + jnp.sum(jnp.where(arrived == wanted, place, 0), axis=1, keepdims=True)
    code = jnp.minimum(code, moved.shape[0] - 1)
    code_v[...] = jnp.broadcast_to(code, code_v.shape)
    code_copy = pltpu.make_async_copy(code_v, code_s, code_sem)
    code_copy.start()
    finish(first)

    def keep(block, state):
        kept[block] = state

    sph(table1, land1, nbr1, sends1, rho1, rho_s1, 2, keep)

    moves = []
    for step, other in enumerate(peers):
        one = jnp.int32(0)
        two = jnp.int32(0)
        for block in reversed(range(blocks)):
            target = slots_s[0, block]
            goes = (target >= other * blocks) & (target < (other + 1) * blocks)
            two = jnp.where(goes, one, two)
            one = jnp.where(goes, block, one)
        out_m[step, 0] = kept[one]
        out_m[step, 1] = kept[two]
        copy = pltpu.make_async_remote_copy(
            src_ref=out_m.at[step],
            dst_ref=moved.at[pl.ds(blocks + MOVE_CAP * step, MOVE_CAP)],
            send_sem=send_g.at[n_group - 1 + step],
            recv_sem=recv_g.at[n_group - 1 + step],
            device_id={"group": other},
            device_id_type=MESH,
        )
        copy.start()
        moves.append(copy)
    code_copy.wait()
    for block in range(blocks):
        moved[block] = kept[block]
    finish(moves)
    for item in range(2 * halo):
        out2[item] = moved[code_s[sends2[0, item], 0]]
    second = exchange(out2, land2, 0, 4)
    for block in range(blocks):
        table2[block] = moved[code_s[block, 0]]
    prepare_own(table2)
    finish(second)

    def emit(block, state):
        for axis in range(3):
            pos_out[0, axis, pl.ds(block, 1), :] = state[axis : axis + 1]
            vel_out[0, axis, pl.ds(block, 1), :] = state[3 + axis : 4 + axis]
        rho_out[0, pl.ds(block, 1), :] = rho2[block]

    sph(table2, land2, nbr2, sends2, rho2, rho_s2, 6, emit)


def body(
    n_curve, n_group,
    positions, velocities, masses, counts, neighbours_first, sends_first, new_slot,
    neighbours_second, sends_second,
):
    blocks, width = masses.shape[1], masses.shape[2]
    halo = sends_first.shape[1] // 2
    whole = blocks + 2 * halo
    peers = n_group - 1
    vmem = pl.BlockSpec(memory_space=pltpu.VMEM)
    smem = pl.BlockSpec(memory_space=pltpu.SMEM)
    scratch = [
        pltpu.VMEM((blocks, 8, width), F32),
        pltpu.VMEM((blocks, 8, width), F32),
        pltpu.VMEM((2 * halo, 8, width), F32),
        pltpu.VMEM((2 * halo, 8, width), F32),
        pltpu.VMEM((blocks, 8, width), F32),
        pltpu.VMEM((blocks + MOVE_CAP * peers, 8, width), F32),
        pltpu.VMEM((2 * halo, 8, width), F32),
        pltpu.VMEM((2 * halo, 8, width), F32),
        pltpu.VMEM((peers, MOVE_CAP, 8, width), F32),
        pltpu.VMEM((whole, 1, width), F32),
        pltpu.VMEM((whole, 1, width), F32),
        pltpu.VMEM((2 * halo, 1, width), F32),
        pltpu.VMEM((2 * halo, 1, width), F32),
        pltpu.VMEM((whole, width, width), BF16),
        pltpu.VMEM((whole, 32, width), BF16),
        pltpu.VMEM((blocks, width, width), BF16),
        pltpu.VMEM((blocks, width, 2 * width), BF16),
        pltpu.VMEM((whole, width, width), F32),
        pltpu.VMEM((whole, width, width), F32),
        pltpu.VMEM((1, width), jnp.int32),
        pltpu.VMEM((peers, 1, width), jnp.int32),
        pltpu.VMEM((blocks, width), jnp.int32),
        pltpu.SMEM((blocks, width), jnp.int32),
        pltpu.SemaphoreType.DMA((8,)),
        pltpu.SemaphoreType.DMA((8,)),
        pltpu.SemaphoreType.DMA((2 * peers,)),
        pltpu.SemaphoreType.DMA((2 * peers,)),
        pltpu.SemaphoreType.DMA,
    ]
    turned = jax.ShapeDtypeStruct((1, 3, blocks, width), F32)
    positions_out, velocities_out, densities_out = pl.pallas_call(
        functools.partial(kernel, n_curve, n_group),
        out_shape=(
            turned,
            turned,
            jax.ShapeDtypeStruct(masses.shape, F32),
        ),
        in_specs=[vmem, vmem, vmem, smem, smem, smem, smem, vmem, smem, smem],
        out_specs=(vmem, vmem, vmem),
        scratch_shapes=scratch,
        compiler_params=pltpu.CompilerParams(
            collective_id=0, has_side_effects=True, vmem_limit_bytes=32 * 1024 * 1024
        ),
        name="sph",
    )(
        positions.transpose(0, 2, 1, 3), velocities.transpose(0, 2, 1, 3), masses, counts,
        neighbours_first.transpose(2, 0, 1), sends_first, new_slot,
        new_slot, neighbours_second.transpose(2, 0, 1), sends_second,
    )
    return (
        positions_out.transpose(0, 2, 1, 3), velocities_out.transpose(0, 2, 1, 3), densities_out,
    )


def solution(mesh):
    blocks4 = P("group", "curve", None, None)
    blocks3 = P("group", "curve", None)
    blocks2 = P("group", "curve")
    in_specs = (
        blocks4, blocks4, blocks3, blocks2, blocks3, blocks2, blocks2, blocks3, blocks2,
    )
    return jax.shard_map(
        functools.partial(body, mesh.shape["curve"], mesh.shape["group"]),
        mesh=mesh, in_specs=in_specs, out_specs=(blocks4, blocks4, blocks3), check_vma=False,
    )
```

```python
import functools
import math

import jax
import jax.numpy as jnp
from jax import lax
from jax.experimental import pallas as pl
from jax.experimental.pallas import tpu as pltpu
from jax.sharding import PartitionSpec as P

KERNEL_SCALE = 4.0
SOFTENING = 0.0025
BACKGROUND = 0.5
TIME_STEP = 0.1
SPACING = 0.6
MOVE_CAP = 2
SCALE = -KERNEL_SCALE
DEAD = -200.0
MESH = pl.DeviceIdType.MESH
F32 = jnp.float32
BF16 = jnp.bfloat16


def split(value):
    high = value.astype(BF16).astype(F32)
    rest = value - high
    middle = rest.astype(BF16).astype(F32)
    return high, middle, rest - middle


def source_rows(value):
    high, middle, low = split(value)
    return [high, middle, low, high, high, middle]


def target_rows(value):
    high, middle, low = split(value)
    return [high, high, high, middle, low, middle]


def rows_of(shape):
    return lax.broadcasted_iota(jnp.int32, shape, 0)


def moments(state, corner):
    row = rows_of(state.shape)
    state = state - jnp.where(row == 0, corner + 0.5, jnp.where(row < 3, 0.5, 0.0))
    square = jnp.sum(jnp.where(row < 3, state * state, 0.0), axis=0, keepdims=True)
    after = pltpu.roll(state, 3, 0)
    cross = jnp.sum(
        jnp.where((row >= 3) & (row < 6), state * after, 0.0), axis=0, keepdims=True
    )
    return row, state, after, square, cross


def prepare_source(state, corner, source_t, source_m):
    row, state, after, square, cross = moments(state, corner)
    mass = state[6:7]
    logm = jnp.where(mass > 0.0, jnp.log(jnp.maximum(mass, 1e-30)), DEAD)
    lower = jnp.where(row < 6, state, jnp.where(row == 6, 1.0, square))
    upper = jnp.where(row == 0, cross, jnp.where(row == 1, logm, 0.0))
    feature = jnp.concatenate([lower, upper], axis=0)
    width = state.shape[1]
    pieces = source_rows(feature)
    used = len(pieces) * feature.shape[0]
    pieces.append(jnp.zeros((width - used, width), F32))
    source_t[...] = jnp.concatenate(pieces, axis=0).astype(BF16).T
    weighted = jnp.where(row < 7, lower * mass, 0.0)
    source_m[...] = jnp.concatenate(
        list(split(weighted)) + [jnp.zeros_like(weighted)], axis=0
    ).astype(BF16)


def prepare_target(state, corner, target_d, target_f):
    row, state, after, square, cross = moments(state, corner)
    width = state.shape[1]
    ahead = pltpu.roll(state, state.shape[0] - 3, 0)
    near = jnp.where(row < 3, (-2.0 * SCALE) * state, 0.0)
    tail = jnp.where(row == 7, SCALE, 0.0)
    plain = jnp.where(row == 6, SCALE * square, near + tail)
    soft = jnp.where(row == 6, SCALE * (square + SOFTENING), near + tail)
    closing = jnp.where(
        row < 3,
        -SCALE * ahead,
        jnp.where(row < 6, -SCALE * after, jnp.where(row == 6, SCALE * cross, 0.0)),
    )
    upper_d = jnp.where(row == 1, 1.0, 0.0)
    upper_c = jnp.where(row == 0, SCALE, 0.0)

    def table(lower, upper):
        pieces = target_rows(jnp.concatenate([lower, upper], axis=0))
        used = len(pieces) * 2 * lower.shape[0]
        pieces.append(jnp.zeros((width - used, width), F32))
        return jnp.concatenate(pieces, axis=0).astype(BF16)

    target_d[...] = table(plain, upper_d)
    target_f[:, 0:width] = table(soft, jnp.zeros_like(upper_c))
    target_f[:, width : 2 * width] = table(closing, upper_c)


def gather(block, nbr, table, axis):
    picks = [block] + [nbr[item, 0, block] for item in range(nbr.shape[0])]
    return picks, jnp.concatenate([table[pick] for pick in picks], axis=axis)


def density_of(block, nbr, source_t, target_d):
    target = target_d[block]
    _, sources = gather(block, nbr, source_t, 0)
    weight = jnp.exp(jnp.dot(sources, target, preferred_element_type=F32))
    return BACKGROUND + jnp.sum(weight, axis=0, keepdims=True)


def force_of(block, nbr, state, corner, rho, rho_col, inv_col, source_t, source_m, target_f):
    width = state.shape[1]
    inverse = 1.0 / rho
    picks, sources = gather(block, nbr, source_t, 0)
    both = jnp.dot(sources, target_f[block], preferred_element_type=F32)
    factors = []
    for item, pick in enumerate(picks):
        part = both[item * width : (item + 1) * width]
        soft = part[:, 0:width]
        closing = jnp.maximum(part[:, width : 2 * width], 0.0)
        bottom = soft * (rho_col[pick] + rho)
        viscous = closing * pl.reciprocal(bottom, approx=True)
        factors.append((jnp.exp(soft) * (inv_col[pick] + inverse - viscous)).astype(BF16))
    _, weighted = gather(block, nbr, source_m, 1)
    total = jnp.dot(weighted, jnp.concatenate(factors, axis=0), preferred_element_type=F32)
    rows = state.shape[0]
    sums = total[0:rows] + total[rows : 2 * rows] + total[2 * rows : 3 * rows]
    row = rows_of(state.shape)
    centred = state - jnp.where(row == 0, corner + 0.5, jnp.where(row < 3, 0.5, 0.0))
    strength = 2.0 * KERNEL_SCALE * math.exp(KERNEL_SCALE * SOFTENING)
    accel = strength * (centred * sums[6:7] - sums)
    velocity = state + TIME_STEP * pltpu.roll(accel, 3, 0)
    position = state + TIME_STEP * pltpu.roll(velocity, rows - 3, 0)
    return jnp.where(row < 3, position, jnp.where(row < 6, velocity, state))


def columns(rho, start, rho_col, inv_col):
    count, _, width = rho.shape
    rows = jnp.concatenate([rho[item] for item in range(count)], axis=0)
    turned = jnp.concatenate([rows, jnp.ones((width - count, width), F32)], axis=0).T
    inverse = 1.0 / turned
    for item in range(count):
        shape = (width, width)
        rho_col[start + item] = jnp.broadcast_to(turned[:, item : item + 1], shape)
        inv_col[start + item] = jnp.broadcast_to(inverse[:, item : item + 1], shape)


def kernel(
    n_curve, n_group,
    pos, vel, mass, counts, nbr1, sends1, slots_s, slots_v, nbr2, sends2,
    pos_out, vel_out, rho_out,
    table1, table2, land1, land2, kept, moved, out1, out2, out_m, rho1, rho2, rho_s1, rho_s2,
    source_t, source_m, target_d, target_f, rho_col, inv_col,
    slots_own, slots_in, code_v, code_s,
    send_sem, recv_sem, send_g, recv_g, code_sem,
):
    blocks = pos.shape[2]
    width = pos.shape[3]
    halo = sends1.shape[1] // 2
    mine = lax.axis_index("curve")
    group = lax.axis_index("group")
    lower = lax.rem(mine + n_curve - 1, n_curve)
    upper = lax.rem(mine + 1, n_curve)
    corner = SPACING * mine.astype(F32)
    barrier = pltpu.get_barrier_semaphore()
    for other in (lower, upper):
        pl.semaphore_signal(barrier, inc=1, device_id={"curve": other}, device_id_type=MESH)
    peers = [lax.rem(group + step, n_group) for step in range(1, n_group)]
    for other in peers:
        pl.semaphore_signal(barrier, inc=1, device_id={"group": other}, device_id_type=MESH)

    lane = lax.broadcasted_iota(jnp.int32, (1, width), 1)

    def load_state(block, carry):
        for axis in range(3):
            table1[block, axis : axis + 1, :] = pos[0, axis, pl.ds(block, 1), :]
            table1[block, 3 + axis : 4 + axis, :] = vel[0, axis, pl.ds(block, 1), :]
        live = jnp.where(lane < counts[0, block], mass[0, pl.ds(block, 1), :], 0.0)
        table1[block, 6:7, :] = live
        table1[block, 7:8, :] = jnp.zeros_like(live)
        return carry

    lax.fori_loop(0, blocks, load_state, 0, unroll=True)
    slots_own[...] = jnp.full(slots_own.shape, -1, jnp.int32)
    slots_own[:, 0:blocks] = slots_v[...]
    for item in range(2 * halo):
        out1[item] = table1[sends1[0, item]]
    pl.semaphore_wait(barrier, 2 + n_group - 1)

    def exchange(outgoing, landing, start, base):
        copies = []
        for side, other in ((0, lower), (1, upper)):
            copies.append(
                pltpu.make_async_remote_copy(
                    src_ref=outgoing.at[pl.ds(side * halo, halo)],
                    dst_ref=landing.at[pl.ds(start + (1 - side) * halo, halo)],
                    send_sem=send_sem.at[base + side],
                    recv_sem=recv_sem.at[base + side],
                    device_id={"curve": other},
                    device_id_type=MESH,
                )
            )
        for copy in copies:
            copy.start()
        return copies

    def finish(copies):
        for copy in copies:
            copy.wait()

    first = exchange(out1, land1, 0, 0)
    lists = []
    for step, other in enumerate(peers):
        copy = pltpu.make_async_remote_copy(
            src_ref=slots_own,
            dst_ref=slots_in.at[step],
            send_sem=send_g.at[step],
            recv_sem=recv_g.at[step],
            device_id={"group": other},
            device_id_type=MESH,
        )
        copy.start()
        lists.append(copy)

    def prepare_own(table):
        def run(block, carry):
            state = table[block]
            prepare_source(state, corner, source_t.at[block], source_m.at[block])
            prepare_target(state, corner, target_d.at[block], target_f.at[block])
            return carry

        lax.fori_loop(0, blocks, run, 0, unroll=8)

    def prepare_halo(land):
        def run(item, carry):
            block = blocks + item
            prepare_source(land[item], corner, source_t.at[block], source_m.at[block])
            return carry

        lax.fori_loop(0, 2 * halo, run, 0, unroll=8)

    def sph(table, land, nbr, sends, rho, rho_send, base, write):
        prepare_halo(land)

        def listed(item, carry):
            rho_send[item] = density_of(sends[0, item], nbr, source_t, target_d)
            return carry

        lax.fori_loop(0, 2 * halo, listed, 0, unroll=4)
        copies = exchange(rho_send, rho, blocks, base)

        def own(block, carry):
            rho[block] = density_of(block, nbr, source_t, target_d)
            return carry

        lax.fori_loop(0, blocks, own, 0, unroll=4)
        columns(rho.at[pl.ds(0, blocks)], 0, rho_col, inv_col)
        finish(copies)
        columns(rho.at[pl.ds(blocks, 2 * halo)], blocks, rho_col, inv_col)

        def push(block, carry):
            write(
                block,
                force_of(
                    block, nbr, table[block], corner, rho[block],
                    rho_col, inv_col, source_t, source_m, target_f,
                ),
            )
            return carry

        lax.fori_loop(0, blocks, push, 0, unroll=2)

    prepare_own(table1)
    finish(lists)
    wanted = rows_of((blocks, width)) + group * blocks
    lanes = lax.broadcasted_iota(jnp.int32, (blocks, width), 1)
    code = jnp.sum(jnp.where(slots_own[...] == wanted, lanes, 0), axis=1, keepdims=True)
    for step in range(n_group - 1):
        arrived = slots_in[step]
        here = (arrived >= group * blocks) & (arrived < (group + 1) * blocks)
        lead = jnp.min(jnp.where(here, lane, width), axis=1, keepdims=True)
        place = blocks + MOVE_CAP * step + jnp.where(lane > lead, 1, 0)
        code = code + jnp.sum(jnp.where(arrived == wanted, place, 0), axis=1, keepdims=True)
    code = jnp.minimum(code, moved.shape[0] - 1)
    code_v[...] = jnp.broadcast_to(code, code_v.shape)
    code_copy = pltpu.make_async_copy(code_v, code_s, code_sem)
    code_copy.start()
    finish(first)

    def keep(block, state):
        kept[block] = state

    sph(table1, land1, nbr1, sends1, rho1, rho_s1, 2, keep)

    moves = []
    for step, other in enumerate(peers):
        one = jnp.int32(0)
        two = jnp.int32(0)
        for block in reversed(range(blocks)):
            target = slots_s[0, block]
            goes = (target >= other * blocks) & (target < (other + 1) * blocks)
            two = jnp.where(goes, one, two)
            one = jnp.where(goes, block, one)
        out_m[step, 0] = kept[one]
        out_m[step, 1] = kept[two]
        copy = pltpu.make_async_remote_copy(
            src_ref=out_m.at[step],
            dst_ref=moved.at[pl.ds(blocks + MOVE_CAP * step, MOVE_CAP)],
            send_sem=send_g.at[n_group - 1 + step],
            recv_sem=recv_g.at[n_group - 1 + step],
            device_id={"group": other},
            device_id_type=MESH,
        )
        copy.start()
        moves.append(copy)
    code_copy.wait()
    for block in range(blocks):
        moved[block] = kept[block]
    finish(moves)
    for item in range(2 * halo):
        out2[item] = moved[code_s[sends2[0, item], 0]]
    second = exchange(out2, land2, 0, 4)
    for block in range(blocks):
        table2[block] = moved[code_s[block, 0]]
    prepare_own(table2)
    finish(second)

    def emit(block, state):
        for axis in range(3):
            pos_out[0, axis, pl.ds(block, 1), :] = state[axis : axis + 1]
            vel_out[0, axis, pl.ds(block, 1), :] = state[3 + axis : 4 + axis]
        rho_out[0, pl.ds(block, 1), :] = rho2[block]

    sph(table2, land2, nbr2, sends2, rho2, rho_s2, 6, emit)


def body(
    n_curve, n_group,
    positions, velocities, masses, counts, neighbours_first, sends_first, new_slot,
    neighbours_second, sends_second,
):
    blocks, width = masses.shape[1], masses.shape[2]
    halo = sends_first.shape[1] // 2
    whole = blocks + 2 * halo
    peers = n_group - 1
    vmem = pl.BlockSpec(memory_space=pltpu.VMEM)
    smem = pl.BlockSpec(memory_space=pltpu.SMEM)
    scratch = [
        pltpu.VMEM((blocks, 8, width), F32),
        pltpu.VMEM((blocks, 8, width), F32),
        pltpu.VMEM((2 * halo, 8, width), F32),
        pltpu.VMEM((2 * halo, 8, width), F32),
        pltpu.VMEM((blocks, 8, width), F32),
        pltpu.VMEM((blocks + MOVE_CAP * peers, 8, width), F32),
        pltpu.VMEM((2 * halo, 8, width), F32),
        pltpu.VMEM((2 * halo, 8, width), F32),
        pltpu.VMEM((peers, MOVE_CAP, 8, width), F32),
        pltpu.VMEM((whole, 1, width), F32),
        pltpu.VMEM((whole, 1, width), F32),
        pltpu.VMEM((2 * halo, 1, width), F32),
        pltpu.VMEM((2 * halo, 1, width), F32),
        pltpu.VMEM((whole, width, width), BF16),
        pltpu.VMEM((whole, 32, width), BF16),
        pltpu.VMEM((blocks, width, width), BF16),
        pltpu.VMEM((blocks, width, 2 * width), BF16),
        pltpu.VMEM((whole, width, width), F32),
        pltpu.VMEM((whole, width, width), F32),
        pltpu.VMEM((1, width), jnp.int32),
        pltpu.VMEM((peers, 1, width), jnp.int32),
        pltpu.VMEM((blocks, width), jnp.int32),
        pltpu.SMEM((blocks, width), jnp.int32),
        pltpu.SemaphoreType.DMA((8,)),
        pltpu.SemaphoreType.DMA((8,)),
        pltpu.SemaphoreType.DMA((2 * peers,)),
        pltpu.SemaphoreType.DMA((2 * peers,)),
        pltpu.SemaphoreType.DMA,
    ]
    turned = jax.ShapeDtypeStruct((1, 3, blocks, width), F32)
    positions_out, velocities_out, densities_out = pl.pallas_call(
        functools.partial(kernel, n_curve, n_group),
        out_shape=(
            turned,
            turned,
            jax.ShapeDtypeStruct(masses.shape, F32),
        ),
        in_specs=[vmem, vmem, vmem, smem, smem, smem, smem, vmem, smem, smem],
        out_specs=(vmem, vmem, vmem),
        scratch_shapes=scratch,
        compiler_params=pltpu.CompilerParams(
            collective_id=0, has_side_effects=True, vmem_limit_bytes=32 * 1024 * 1024
        ),
        name="sph",
    )(
        positions.transpose(0, 2, 1, 3), velocities.transpose(0, 2, 1, 3), masses, counts,
        neighbours_first.transpose(2, 0, 1), sends_first, new_slot,
        new_slot, neighbours_second.transpose(2, 0, 1), sends_second,
    )
    return (
        positions_out.transpose(0, 2, 1, 3), velocities_out.transpose(0, 2, 1, 3), densities_out,
    )


def solution(mesh):
    blocks4 = P("group", "curve", None, None)
    blocks3 = P("group", "curve", None)
    blocks2 = P("group", "curve")
    in_specs = (
        blocks4, blocks4, blocks3, blocks2, blocks3, blocks2, blocks2, blocks3, blocks2,
    )
    return jax.shard_map(
        functools.partial(body, mesh.shape["curve"], mesh.shape["group"]),
        mesh=mesh, in_specs=in_specs, out_specs=(blocks4, blocks4, blocks3), check_vma=False,
    )
```

```python
import functools
import math

import jax
import jax.numpy as jnp
from jax import lax
from jax.experimental import pallas as pl
from jax.experimental.pallas import tpu as pltpu
from jax.sharding import PartitionSpec as P

KERNEL_SCALE = 4.0
SOFTENING = 0.0025
BACKGROUND = 0.5
TIME_STEP = 0.1
SPACING = 0.6
MOVE_CAP = 2
SCALE = -KERNEL_SCALE
MESH = pl.DeviceIdType.MESH
F32 = jnp.float32
BF16 = jnp.bfloat16


def split(value):
    high = value.astype(BF16).astype(F32)
    rest = value - high
    middle = rest.astype(BF16).astype(F32)
    return high, middle, rest - middle


def source_rows(value):
    high, middle, low = split(value)
    return [high, middle, low, high, high, middle]


def target_rows(value):
    high, middle, low = split(value)
    return [high, high, high, middle, low, middle]


def rows_of(shape):
    return lax.broadcasted_iota(jnp.int32, shape, 0)


def moments(state, corner):
    row = rows_of(state.shape)
    state = state - jnp.where(row == 0, corner + 0.5, jnp.where(row < 3, 0.5, 0.0))
    square = jnp.sum(jnp.where(row < 3, state * state, 0.0), axis=0, keepdims=True)
    after = pltpu.roll(state, 3, 0)
    cross = jnp.sum(
        jnp.where((row >= 3) & (row < 6), state * after, 0.0), axis=0, keepdims=True
    )
    return row, state, after, square, cross


def prepare_source(state, corner, source_t):
    row, state, after, square, cross = moments(state, corner)
    lower = jnp.where(row < 6, state, jnp.where(row == 6, 1.0, square))
    upper = jnp.where(row == 0, cross, 0.0)
    pieces = source_rows(jnp.concatenate([lower, upper], axis=0))
    width = state.shape[1]
    used = len(pieces) * 2 * state.shape[0]
    pieces.append(jnp.zeros((width - used, width), F32))
    source_t[...] = jnp.concatenate(pieces, axis=0).astype(BF16).T


def prepare_target(state, corner, target):
    row, state, after, square, cross = moments(state, corner)
    width = state.shape[1]
    ahead = pltpu.roll(state, state.shape[0] - 3, 0)
    soft = jnp.where(
        row < 3,
        (-2.0 * SCALE) * state,
        jnp.where(
            row == 6, SCALE * (square + SOFTENING), jnp.where(row == 7, SCALE, 0.0)
        ),
    )
    closing = jnp.where(
        row < 3,
        -SCALE * ahead,
        jnp.where(row < 6, -SCALE * after, jnp.where(row == 6, SCALE * cross, 0.0)),
    )
    upper = jnp.where(row == 0, SCALE, 0.0)

    def table(low, high):
        pieces = target_rows(jnp.concatenate([low, high], axis=0))
        used = len(pieces) * 2 * low.shape[0]
        pieces.append(jnp.zeros((width - used, width), F32))
        return jnp.concatenate(pieces, axis=0).astype(BF16)

    target[:, 0:width] = table(soft, jnp.zeros_like(upper))
    target[:, width : 2 * width] = table(closing, upper)


def prepare_weights(state, corner, rho, source_m):
    row = rows_of(state.shape)
    mass = state[6:7]
    centred = state - jnp.where(row == 0, corner + 0.5, jnp.where(row < 3, 0.5, 0.0))
    weighted = jnp.where(row < 3, centred, jnp.where(row == 6, 1.0, 0.0)) * mass
    both = jnp.concatenate([weighted, weighted * (1.0 / rho)], axis=0)
    source_m[...] = jnp.concatenate(list(split(both)), axis=0).astype(BF16)


def gather(block, nbr, table, axis):
    picks = [block] + [nbr[item, 0, block] for item in range(nbr.shape[0])]
    return picks, jnp.concatenate([table[pick] for pick in picks], axis=axis)


LIFT = math.exp(KERNEL_SCALE * SOFTENING)


def listed_density(block, nbr, source_t, target, mass_col):
    width = mass_col.shape[-1]
    picks, sources = gather(block, nbr, source_t, 0)
    soft = jnp.dot(sources, target[block][:, 0:width], preferred_element_type=F32)
    total = None
    for item, pick in enumerate(picks):
        term = jnp.exp(soft[item * width : (item + 1) * width]) * mass_col[pick]
        total = term if total is None else total + term
    return BACKGROUND + LIFT * jnp.sum(total, axis=0, keepdims=True)


def own_density(block, nbr, source_t, target, mass_col, weights, drags):
    width = mass_col.shape[-1]
    picks, sources = gather(block, nbr, source_t, 0)
    both = jnp.dot(sources, target[block], preferred_element_type=F32)
    total = None
    for item, pick in enumerate(picks):
        span = slice(item * width, (item + 1) * width)
        soft = both[span, 0:width]
        closing = jnp.maximum(both[span, width : 2 * width], 0.0)
        weight = jnp.exp(soft)
        term = weight * mass_col[pick]
        total = term if total is None else total + term
        weights[block, span, :] = weight.astype(BF16)
        drags[block, span, :] = weight * (closing * pl.reciprocal(soft, approx=True))
    return BACKGROUND + LIFT * jnp.sum(total, axis=0, keepdims=True)


def force_of(block, nbr, state, corner, rho, rho_col, source_m, weights, drags):
    width = state.shape[1]
    picks, weighted = gather(block, nbr, source_m, 1)
    parts = []
    for item, pick in enumerate(picks):
        drag = drags[block, item * width : (item + 1) * width, :]
        parts.append((drag * pl.reciprocal(rho_col[pick] + rho, approx=True)).astype(BF16))
    right = jnp.concatenate([weights[block], jnp.concatenate(parts, axis=0)], axis=1)
    total = jnp.dot(weighted, right, preferred_element_type=F32)
    rows = state.shape[0]
    total = total[0 : 2 * rows] + total[2 * rows : 4 * rows] + total[4 * rows : 6 * rows]
    sums = (
        total[0:rows, 0:width] * (1.0 / rho)
        + total[rows : 2 * rows, 0:width]
        - total[0:rows, width : 2 * width]
    )
    row = rows_of(state.shape)
    centred = state - jnp.where(row == 0, corner + 0.5, jnp.where(row < 3, 0.5, 0.0))
    accel = (2.0 * KERNEL_SCALE * LIFT) * (centred * sums[6:7] - sums)
    velocity = state + TIME_STEP * pltpu.roll(accel, 3, 0)
    position = state + TIME_STEP * pltpu.roll(velocity, rows - 3, 0)
    return jnp.where(row < 3, position, jnp.where(row < 6, velocity, state))


def columns(rows, start, col):
    count, width = len(rows), rows[0].shape[1]
    rows = jnp.concatenate(rows, axis=0)
    turned = jnp.concatenate([rows, jnp.zeros((width - count, width), F32)], axis=0).T
    for item in range(count):
        col[start + item] = jnp.broadcast_to(turned[:, item : item + 1], (width, width))


def kernel(
    n_curve, n_group,
    pos, vel, mass, counts, nbr1, sends1, slots_s, slots_v, nbr2, sends2,
    pos_out, vel_out, rho_out,
    table1, table2, land1, land2, kept, moved, out1, out2, out_m, rho1, rho2, rho_s1, rho_s2,
    source_t, source_m, target, rho_col, mass_col, weights, drags,
    slots_own, slots_in, code_v, code_s,
    send_sem, recv_sem, send_g, recv_g, code_sem,
):
    blocks = pos.shape[2]
    width = pos.shape[3]
    halo = sends1.shape[1] // 2
    mine = lax.axis_index("curve")
    group = lax.axis_index("group")
    lower = lax.rem(mine + n_curve - 1, n_curve)
    upper = lax.rem(mine + 1, n_curve)
    corner = SPACING * mine.astype(F32)
    barrier = pltpu.get_barrier_semaphore()
    for other in (lower, upper):
        pl.semaphore_signal(barrier, inc=1, device_id={"curve": other}, device_id_type=MESH)
    peers = [lax.rem(group + step, n_group) for step in range(1, n_group)]
    for other in peers:
        pl.semaphore_signal(barrier, inc=1, device_id={"group": other}, device_id_type=MESH)

    lane = lax.broadcasted_iota(jnp.int32, (1, width), 1)

    def load_state(block, carry):
        for axis in range(3):
            table1[block, axis : axis + 1, :] = pos[0, axis, pl.ds(block, 1), :]
            table1[block, 3 + axis : 4 + axis, :] = vel[0, axis, pl.ds(block, 1), :]
        live = jnp.where(lane < counts[0, block], mass[0, pl.ds(block, 1), :], 0.0)
        table1[block, 6:7, :] = live
        table1[block, 7:8, :] = jnp.zeros_like(live)
        return carry

    lax.fori_loop(0, blocks, load_state, 0, unroll=True)
    slots_own[...] = jnp.full(slots_own.shape, -1, jnp.int32)
    slots_own[:, 0:blocks] = slots_v[...]
    for item in range(2 * halo):
        out1[item] = table1[sends1[0, item]]
    pl.semaphore_wait(barrier, 2 + n_group - 1)

    def exchange(outgoing, landing, start, base):
        copies = []
        for side, other in ((0, lower), (1, upper)):
            copies.append(
                pltpu.make_async_remote_copy(
                    src_ref=outgoing.at[pl.ds(side * halo, halo)],
                    dst_ref=landing.at[pl.ds(start + (1 - side) * halo, halo)],
                    send_sem=send_sem.at[base + side],
                    recv_sem=recv_sem.at[base + side],
                    device_id={"curve": other},
                    device_id_type=MESH,
                )
            )
        for copy in copies:
            copy.start()
        return copies

    def finish(copies):
        for copy in copies:
            copy.wait()

    first = exchange(out1, land1, 0, 0)
    lists = []
    for step, other in enumerate(peers):
        copy = pltpu.make_async_remote_copy(
            src_ref=slots_own,
            dst_ref=slots_in.at[step],
            send_sem=send_g.at[step],
            recv_sem=recv_g.at[step],
            device_id={"group": other},
            device_id_type=MESH,
        )
        copy.start()
        lists.append(copy)

    def prepare_own(table):
        def run(block, carry):
            state = table[block]
            prepare_source(state, corner, source_t.at[block])
            prepare_target(state, corner, target.at[block])
            return carry

        lax.fori_loop(0, blocks, run, 0, unroll=8)
        columns([table[block, 6:7, :] for block in range(blocks)], 0, mass_col)

    def prepare_halo(land):
        def run(item, carry):
            prepare_source(land[item], corner, source_t.at[blocks + item])
            return carry

        lax.fori_loop(0, 2 * halo, run, 0, unroll=8)
        columns([land[item, 6:7, :] for item in range(2 * halo)], blocks, mass_col)

    def sph(table, land, nbr, sends, rho, rho_send, base, write):
        prepare_halo(land)

        def listed(item, carry):
            rho_send[item] = listed_density(sends[0, item], nbr, source_t, target, mass_col)
            return carry

        lax.fori_loop(0, 2 * halo, listed, 0, unroll=4)
        copies = exchange(rho_send, rho, blocks, base)

        def own(block, carry):
            rho[block] = own_density(
                block, nbr, source_t, target, mass_col, weights, drags
            )
            return carry

        lax.fori_loop(0, blocks, own, 0, unroll=2)
        def weigh(block, carry):
            prepare_weights(table[block], corner, rho[block], source_m.at[block])
            return carry

        lax.fori_loop(0, blocks, weigh, 0, unroll=4)
        columns([rho[block] for block in range(blocks)], 0, rho_col)
        finish(copies)
        columns([rho[blocks + item] for item in range(2 * halo)], blocks, rho_col)

        def weigh_halo(item, carry):
            block = blocks + item
            prepare_weights(land[item], corner, rho[block], source_m.at[block])
            return carry

        lax.fori_loop(0, 2 * halo, weigh_halo, 0, unroll=4)

        def push(block, carry):
            write(
                block,
                force_of(
                    block, nbr, table[block], corner, rho[block],
                    rho_col, source_m, weights, drags,
                ),
            )
            return carry

        lax.fori_loop(0, blocks, push, 0, unroll=2)

    prepare_own(table1)
    finish(lists)
    wanted = rows_of((blocks, width)) + group * blocks
    lanes = lax.broadcasted_iota(jnp.int32, (blocks, width), 1)
    code = jnp.sum(jnp.where(slots_own[...] == wanted, lanes, 0), axis=1, keepdims=True)
    for step in range(n_group - 1):
        arrived = slots_in[step]
        here = (arrived >= group * blocks) & (arrived < (group + 1) * blocks)
        lead = jnp.min(jnp.where(here, lane, width), axis=1, keepdims=True)
        place = blocks + MOVE_CAP * step + jnp.where(lane > lead, 1, 0)
        code = code + jnp.sum(jnp.where(arrived == wanted, place, 0), axis=1, keepdims=True)
    code = jnp.minimum(code, moved.shape[0] - 1)
    code_v[...] = jnp.broadcast_to(code, code_v.shape)
    code_copy = pltpu.make_async_copy(code_v, code_s, code_sem)
    code_copy.start()
    finish(first)

    def keep(block, state):
        kept[block] = state

    sph(table1, land1, nbr1, sends1, rho1, rho_s1, 2, keep)

    moves = []
    for step, other in enumerate(peers):
        one = jnp.int32(0)
        two = jnp.int32(0)
        for block in reversed(range(blocks)):
            owner = slots_s[0, block]
            goes = (owner >= other * blocks) & (owner < (other + 1) * blocks)
            two = jnp.where(goes, one, two)
            one = jnp.where(goes, block, one)
        out_m[step, 0] = kept[one]
        out_m[step, 1] = kept[two]
        copy = pltpu.make_async_remote_copy(
            src_ref=out_m.at[step],
            dst_ref=moved.at[pl.ds(blocks + MOVE_CAP * step, MOVE_CAP)],
            send_sem=send_g.at[n_group - 1 + step],
            recv_sem=recv_g.at[n_group - 1 + step],
            device_id={"group": other},
            device_id_type=MESH,
        )
        copy.start()
        moves.append(copy)
    code_copy.wait()
    for block in range(blocks):
        moved[block] = kept[block]
    finish(moves)
    for item in range(2 * halo):
        out2[item] = moved[code_s[sends2[0, item], 0]]
    second = exchange(out2, land2, 0, 4)
    for block in range(blocks):
        table2[block] = moved[code_s[block, 0]]
    prepare_own(table2)
    finish(second)

    def emit(block, state):
        for axis in range(3):
            pos_out[0, axis, pl.ds(block, 1), :] = state[axis : axis + 1]
            vel_out[0, axis, pl.ds(block, 1), :] = state[3 + axis : 4 + axis]
        rho_out[0, pl.ds(block, 1), :] = rho2[block]

    sph(table2, land2, nbr2, sends2, rho2, rho_s2, 6, emit)


def body(
    n_curve, n_group,
    positions, velocities, masses, counts, neighbours_first, sends_first, new_slot,
    neighbours_second, sends_second,
):
    blocks, width = masses.shape[1], masses.shape[2]
    halo = sends_first.shape[1] // 2
    whole = blocks + 2 * halo
    peers = n_group - 1
    sources = neighbours_first.shape[2] + 1
    vmem = pl.BlockSpec(memory_space=pltpu.VMEM)
    smem = pl.BlockSpec(memory_space=pltpu.SMEM)
    scratch = [
        pltpu.VMEM((blocks, 8, width), F32),
        pltpu.VMEM((blocks, 8, width), F32),
        pltpu.VMEM((2 * halo, 8, width), F32),
        pltpu.VMEM((2 * halo, 8, width), F32),
        pltpu.VMEM((blocks, 8, width), F32),
        pltpu.VMEM((blocks + MOVE_CAP * peers, 8, width), F32),
        pltpu.VMEM((2 * halo, 8, width), F32),
        pltpu.VMEM((2 * halo, 8, width), F32),
        pltpu.VMEM((peers, MOVE_CAP, 8, width), F32),
        pltpu.VMEM((whole, 1, width), F32),
        pltpu.VMEM((whole, 1, width), F32),
        pltpu.VMEM((2 * halo, 1, width), F32),
        pltpu.VMEM((2 * halo, 1, width), F32),
        pltpu.VMEM((whole, width, width), BF16),
        pltpu.VMEM((whole, 48, width), BF16),
        pltpu.VMEM((blocks, width, 2 * width), BF16),
        pltpu.VMEM((whole, width, width), F32),
        pltpu.VMEM((whole, width, width), F32),
        pltpu.VMEM((blocks, sources * width, width), BF16),
        pltpu.VMEM((blocks, sources * width, width), F32),
        pltpu.VMEM((1, width), jnp.int32),
        pltpu.VMEM((peers, 1, width), jnp.int32),
        pltpu.VMEM((blocks, width), jnp.int32),
        pltpu.SMEM((blocks, width), jnp.int32),
        pltpu.SemaphoreType.DMA((8,)),
        pltpu.SemaphoreType.DMA((8,)),
        pltpu.SemaphoreType.DMA((2 * peers,)),
        pltpu.SemaphoreType.DMA((2 * peers,)),
        pltpu.SemaphoreType.DMA,
    ]
    turned = jax.ShapeDtypeStruct((1, 3, blocks, width), F32)
    positions_out, velocities_out, densities_out = pl.pallas_call(
        functools.partial(kernel, n_curve, n_group),
        out_shape=(
            turned,
            turned,
            jax.ShapeDtypeStruct(masses.shape, F32),
        ),
        in_specs=[vmem, vmem, vmem, smem, smem, smem, smem, vmem, smem, smem],
        out_specs=(vmem, vmem, vmem),
        scratch_shapes=scratch,
        compiler_params=pltpu.CompilerParams(
            collective_id=0, has_side_effects=True, vmem_limit_bytes=56 * 1024 * 1024
        ),
        name="sph",
    )(
        positions.transpose(0, 2, 1, 3), velocities.transpose(0, 2, 1, 3), masses, counts,
        neighbours_first.transpose(2, 0, 1), sends_first, new_slot,
        new_slot, neighbours_second.transpose(2, 0, 1), sends_second,
    )
    return (
        positions_out.transpose(0, 2, 1, 3), velocities_out.transpose(0, 2, 1, 3), densities_out,
    )


def solution(mesh):
    blocks4 = P("group", "curve", None, None)
    blocks3 = P("group", "curve", None)
    blocks2 = P("group", "curve")
    in_specs = (
        blocks4, blocks4, blocks3, blocks2, blocks3, blocks2, blocks2, blocks3, blocks2,
    )
    return jax.shard_map(
        functools.partial(body, mesh.shape["curve"], mesh.shape["group"]),
        mesh=mesh, in_specs=in_specs, out_specs=(blocks4, blocks4, blocks3), check_vma=False,
    )
```

```python
import functools
import math

import jax
import jax.numpy as jnp
from jax import lax
from jax.experimental import pallas as pl
from jax.experimental.pallas import tpu as pltpu
from jax.sharding import PartitionSpec as P

KERNEL_SCALE = 4.0
SOFTENING = 0.0025
BACKGROUND = 0.5
TIME_STEP = 0.1
SPACING = 0.6
MOVE_CAP = 2
SCALE = -KERNEL_SCALE
MESH = pl.DeviceIdType.MESH
F32 = jnp.float32
BF16 = jnp.bfloat16


def split(value):
    high = value.astype(BF16).astype(F32)
    rest = value - high
    middle = rest.astype(BF16).astype(F32)
    return high, middle, rest - middle


def source_rows(value):
    high, middle, low = split(value)
    return [high, middle, low, high, high, middle]


def target_rows(value):
    high, middle, low = split(value)
    return [high, high, high, middle, low, middle]


def rows_of(shape):
    return lax.broadcasted_iota(jnp.int32, shape, 0)


def moments(state, corner):
    row = rows_of(state.shape)
    state = state - jnp.where(row == 0, corner + 0.5, jnp.where(row < 3, 0.5, 0.0))
    square = jnp.sum(jnp.where(row < 3, state * state, 0.0), axis=0, keepdims=True)
    after = pltpu.roll(state, 3, 0)
    cross = jnp.sum(
        jnp.where((row >= 3) & (row < 6), state * after, 0.0), axis=0, keepdims=True
    )
    return row, state, after, square, cross


def prepare_source(state, corner, source_t):
    row, state, after, square, cross = moments(state, corner)
    lower = jnp.where(row < 6, state, jnp.where(row == 6, 1.0, square))
    upper = jnp.where(row == 0, cross, 0.0)
    pieces = source_rows(jnp.concatenate([lower, upper], axis=0))
    width = state.shape[1]
    used = len(pieces) * 2 * state.shape[0]
    pieces.append(jnp.zeros((width - used, width), F32))
    source_t[...] = jnp.concatenate(pieces, axis=0).astype(BF16).T


def prepare_target(state, corner, target):
    row, state, after, square, cross = moments(state, corner)
    width = state.shape[1]
    ahead = pltpu.roll(state, state.shape[0] - 3, 0)
    soft = jnp.where(
        row < 3,
        (-2.0 * SCALE) * state,
        jnp.where(
            row == 6, SCALE * (square + SOFTENING), jnp.where(row == 7, SCALE, 0.0)
        ),
    )
    closing = jnp.where(
        row < 3,
        -SCALE * ahead,
        jnp.where(row < 6, -SCALE * after, jnp.where(row == 6, SCALE * cross, 0.0)),
    )
    upper = jnp.where(row == 0, SCALE, 0.0)

    def table(low, high):
        pieces = target_rows(jnp.concatenate([low, high], axis=0))
        used = len(pieces) * 2 * low.shape[0]
        pieces.append(jnp.zeros((width - used, width), F32))
        return jnp.concatenate(pieces, axis=0).astype(BF16)

    target[:, 0:width] = table(soft, jnp.zeros_like(upper))
    target[:, width : 2 * width] = table(closing, upper)


def prepare_weights(state, corner, rho, source_m):
    row = rows_of(state.shape)
    mass = state[6:7]
    centred = state - jnp.where(row == 0, corner + 0.5, jnp.where(row < 3, 0.5, 0.0))
    weighted = jnp.where(row < 3, centred, jnp.where(row == 6, 1.0, 0.0)) * mass
    both = jnp.concatenate([weighted, weighted * (1.0 / rho)], axis=0)
    source_m[...] = jnp.concatenate(list(split(both)), axis=0).astype(BF16)


def gather(block, nbr, table, axis, place):
    picks = [block] + [nbr[item, 0, block] for item in range(nbr.shape[0])]
    picks = [place(pick) for pick in picks]
    return picks, jnp.concatenate([table[pick] for pick in picks], axis=axis)


LIFT = math.exp(KERNEL_SCALE * SOFTENING)


def listed_density(block, nbr, source_t, target, mass_col, place):
    width = mass_col.shape[-1]
    picks, sources = gather(block, nbr, source_t, 0, place)
    soft = jnp.dot(sources, target[place(block), :, 0:width], preferred_element_type=F32)
    total = None
    for item, pick in enumerate(picks):
        term = jnp.exp(soft[item * width : (item + 1) * width]) * mass_col[pick]
        total = term if total is None else total + term
    return BACKGROUND + LIFT * jnp.sum(total, axis=0, keepdims=True)


def own_density(block, nbr, source_t, target, mass_col, weights, drags, place):
    width = mass_col.shape[-1]
    picks, sources = gather(block, nbr, source_t, 0, place)
    both = jnp.dot(sources, target[place(block)], preferred_element_type=F32)
    total = None
    for item, pick in enumerate(picks):
        span = slice(item * width, (item + 1) * width)
        soft = both[span, 0:width]
        closing = jnp.maximum(both[span, width : 2 * width], 0.0)
        weight = jnp.exp(soft)
        term = weight * mass_col[pick]
        total = term if total is None else total + term
        weights[block, span, :] = weight.astype(BF16)
        drags[block, span, :] = weight * (closing * pl.reciprocal(soft, approx=True))
    return BACKGROUND + LIFT * jnp.sum(total, axis=0, keepdims=True)


def force_of(block, nbr, state, corner, rho, rho_col, source_m, weights, drags):
    width = state.shape[1]
    picks, weighted = gather(block, nbr, source_m, 1, lambda pick: pick)
    parts = []
    for item, pick in enumerate(picks):
        drag = drags[block, item * width : (item + 1) * width, :]
        parts.append((drag * pl.reciprocal(rho_col[pick] + rho, approx=True)).astype(BF16))
    right = jnp.concatenate([weights[block], jnp.concatenate(parts, axis=0)], axis=1)
    total = jnp.dot(weighted, right, preferred_element_type=F32)
    rows = state.shape[0]
    total = total[0 : 2 * rows] + total[2 * rows : 4 * rows] + total[4 * rows : 6 * rows]
    sums = (
        total[0:rows, 0:width] * (1.0 / rho)
        + total[rows : 2 * rows, 0:width]
        - total[0:rows, width : 2 * width]
    )
    row = rows_of(state.shape)
    centred = state - jnp.where(row == 0, corner + 0.5, jnp.where(row < 3, 0.5, 0.0))
    accel = (2.0 * KERNEL_SCALE * LIFT) * (centred * sums[6:7] - sums)
    velocity = state + TIME_STEP * pltpu.roll(accel, 3, 0)
    position = state + TIME_STEP * pltpu.roll(velocity, rows - 3, 0)
    return jnp.where(row < 3, position, jnp.where(row < 6, velocity, state))


def columns(rows, start, col):
    count, width = len(rows), rows[0].shape[1]
    rows = jnp.concatenate(rows, axis=0)
    turned = jnp.concatenate([rows, jnp.zeros((width - count, width), F32)], axis=0).T
    for item in range(count):
        col[start + item] = jnp.broadcast_to(turned[:, item : item + 1], (width, width))


def kernel(
    n_curve, n_group,
    pos_h, vel_h, mass_h, counts_h, nbr1_h, sends1_h, slots_h, nbr2_h, sends2_h,
    pos_out, vel_out, rho_out,
    pos, vel, mass, counts, nbr1, sends1, slots_s, slots_v, nbr2, sends2, in_sem,
    table1, table2, land1, land2, kept, moved, out1, out2, out_m, rho1, rho2, rho_s1, rho_s2,
    source_t, source_m, target, rho_col, mass_col, weights, drags,
    slots_own, slots_in, code_v, code_s,
    send_sem, recv_sem, send_g, recv_g, code_sem,
):
    blocks = pos.shape[2]
    width = pos.shape[3]
    halo = sends1.shape[1] // 2
    mine = lax.axis_index("curve")
    group = lax.axis_index("group")
    lower = lax.rem(mine + n_curve - 1, n_curve)
    upper = lax.rem(mine + 1, n_curve)
    corner = SPACING * mine.astype(F32)
    barrier = pltpu.get_barrier_semaphore()
    for other in (lower, upper):
        pl.semaphore_signal(barrier, inc=1, device_id={"curve": other}, device_id_type=MESH)
    peers = [lax.rem(group + step, n_group) for step in range(1, n_group)]
    for other in peers:
        pl.semaphore_signal(barrier, inc=1, device_id={"group": other}, device_id_type=MESH)

    loads = [
        pltpu.make_async_copy(source, landing, in_sem.at[item])
        for item, (source, landing) in enumerate(
            (
                (pos_h, pos), (vel_h, vel), (mass_h, mass), (counts_h, counts),
                (sends1_h, sends1), (slots_h, slots_v), (slots_h, slots_s),
                (nbr1_h, nbr1), (nbr2_h, nbr2), (sends2_h, sends2),
            )
        )
    ]
    for load in loads:
        load.start()
    lane = lax.broadcasted_iota(jnp.int32, (1, width), 1)
    for load in loads:
        load.wait()

    def load_state(block, carry):
        for axis in range(3):
            table1[block, axis : axis + 1, :] = pos[0, axis, pl.ds(block, 1), :]
            table1[block, 3 + axis : 4 + axis, :] = vel[0, axis, pl.ds(block, 1), :]
        live = jnp.where(lane < counts[0, block], mass[0, pl.ds(block, 1), :], 0.0)
        table1[block, 6:7, :] = live
        table1[block, 7:8, :] = jnp.zeros_like(live)
        return carry

    lax.fori_loop(0, blocks, load_state, 0, unroll=True)
    slots_own[...] = jnp.full(slots_own.shape, -1, jnp.int32)
    slots_own[:, 0:blocks] = slots_v[...]
    for item in range(2 * halo):
        out1[item] = table1[sends1[0, item]]
    pl.semaphore_wait(barrier, 2 + n_group - 1)

    def exchange(outgoing, landing, start, base):
        copies = []
        for side, other in ((0, lower), (1, upper)):
            copies.append(
                pltpu.make_async_remote_copy(
                    src_ref=outgoing.at[pl.ds(side * halo, halo)],
                    dst_ref=landing.at[pl.ds(start + (1 - side) * halo, halo)],
                    send_sem=send_sem.at[base + side],
                    recv_sem=recv_sem.at[base + side],
                    device_id={"curve": other},
                    device_id_type=MESH,
                )
            )
        for copy in copies:
            copy.start()
        return copies

    def finish(copies):
        for copy in copies:
            copy.wait()

    first = exchange(out1, land1, 0, 0)
    lists = []
    for step, other in enumerate(peers):
        copy = pltpu.make_async_remote_copy(
            src_ref=slots_own,
            dst_ref=slots_in.at[step],
            send_sem=send_g.at[step],
            recv_sem=recv_g.at[step],
            device_id={"group": other},
            device_id_type=MESH,
        )
        copy.start()
        lists.append(copy)

    def prepare(table, start, count, offset):
        def run(item, carry):
            state = table[start + item]
            prepare_source(state, corner, source_t.at[offset + item])
            prepare_target(state, corner, target.at[offset + item])
            return carry

        lax.fori_loop(0, count, run, 0, unroll=8)
        rows = [table[start + item, 6:7, :] for item in range(count)]
        columns(rows, offset, mass_col)

    def prepare_halo(land, offset):
        def run(item, carry):
            prepare_source(land[item], corner, source_t.at[offset + item])
            return carry

        lax.fori_loop(0, 2 * halo, run, 0, unroll=8)
        columns([land[item, 6:7, :] for item in range(2 * halo)], offset, mass_col)

    def sph(table, land, nbr, sends, rho, rho_send, base, offset, place, write):
        prepare_halo(land, offset)

        def listed(item, carry):
            rho_send[item] = listed_density(
                sends[0, item], nbr, source_t, target, mass_col, place
            )
            return carry

        lax.fori_loop(0, 2 * halo, listed, 0, unroll=4)
        copies = exchange(rho_send, rho, blocks, base)

        def own(block, carry):
            rho[block] = own_density(
                block, nbr, source_t, target, mass_col, weights, drags, place
            )
            return carry

        lax.fori_loop(0, blocks, own, 0, unroll=2)
        def weigh(block, carry):
            prepare_weights(table[block], corner, rho[block], source_m.at[block])
            return carry

        lax.fori_loop(0, blocks, weigh, 0, unroll=4)
        columns([rho[block] for block in range(blocks)], 0, rho_col)
        finish(copies)
        columns([rho[blocks + item] for item in range(2 * halo)], blocks, rho_col)

        def weigh_halo(item, carry):
            block = blocks + item
            prepare_weights(land[item], corner, rho[block], source_m.at[block])
            return carry

        lax.fori_loop(0, 2 * halo, weigh_halo, 0, unroll=4)

        def push(block, carry):
            write(
                block,
                force_of(
                    block, nbr, table[block], corner, rho[block],
                    rho_col, source_m, weights, drags,
                ),
            )
            return carry

        lax.fori_loop(0, blocks, push, 0, unroll=2)

    prepare(table1, 0, blocks, 0)
    finish(lists)
    wanted = rows_of((blocks, width)) + group * blocks
    lanes = lax.broadcasted_iota(jnp.int32, (blocks, width), 1)
    code = jnp.sum(jnp.where(slots_own[...] == wanted, lanes, 0), axis=1, keepdims=True)
    for step in range(n_group - 1):
        arrived = slots_in[step]
        here = (arrived >= group * blocks) & (arrived < (group + 1) * blocks)
        lead = jnp.min(jnp.where(here, lane, width), axis=1, keepdims=True)
        place = blocks + MOVE_CAP * step + jnp.where(lane > lead, 1, 0)
        code = code + jnp.sum(jnp.where(arrived == wanted, place, 0), axis=1, keepdims=True)
    code = jnp.minimum(code, moved.shape[0] - 1)
    code_v[0:blocks, :] = jnp.broadcast_to(code, (blocks, width))
    code_v[blocks:, :] = moved.shape[0] + rows_of((2 * halo, width))
    code_copy = pltpu.make_async_copy(code_v, code_s, code_sem)
    code_copy.start()
    finish(first)

    def keep(block, state):
        kept[block] = state

    sph(table1, land1, nbr1, sends1, rho1, rho_s1, 2, blocks, lambda pick: pick, keep)

    moves_in = MOVE_CAP * (n_group - 1)
    moves = []
    for step, other in enumerate(peers):
        one = jnp.int32(0)
        two = jnp.int32(0)
        for block in reversed(range(blocks)):
            owner = slots_s[0, block]
            goes = (owner >= other * blocks) & (owner < (other + 1) * blocks)
            two = jnp.where(goes, one, two)
            one = jnp.where(goes, block, one)
        out_m[step, 0] = kept[one]
        out_m[step, 1] = kept[two]
        copy = pltpu.make_async_remote_copy(
            src_ref=out_m.at[step],
            dst_ref=moved.at[pl.ds(blocks + MOVE_CAP * step, MOVE_CAP)],
            send_sem=send_g.at[n_group - 1 + step],
            recv_sem=recv_g.at[n_group - 1 + step],
            device_id={"group": other},
            device_id_type=MESH,
        )
        copy.start()
        moves.append(copy)
    code_copy.wait()
    for block in range(blocks):
        moved[block] = kept[block]
    prepare(kept, 0, blocks, 0)
    finish(moves)
    for item in range(2 * halo):
        out2[item] = moved[code_s[sends2[0, item], 0]]
    second = exchange(out2, land2, 0, 4)
    for block in range(blocks):
        table2[block] = moved[code_s[block, 0]]
    prepare(moved, blocks, moves_in, blocks)
    finish(second)

    def emit(block, state):
        for axis in range(3):
            pos_out[0, axis, pl.ds(block, 1), :] = state[axis : axis + 1]
            vel_out[0, axis, pl.ds(block, 1), :] = state[3 + axis : 4 + axis]
        rho_out[0, pl.ds(block, 1), :] = rho2[block]

    sph(
        table2, land2, nbr2, sends2, rho2, rho_s2, 6, blocks + moves_in,
        lambda pick: code_s[pick, 0], emit,
    )


def body(
    n_curve, n_group,
    positions, velocities, masses, counts, neighbours_first, sends_first, new_slot,
    neighbours_second, sends_second,
):
    blocks, width = masses.shape[1], masses.shape[2]
    halo = sends_first.shape[1] // 2
    whole = blocks + 2 * halo
    peers = n_group - 1
    sources = neighbours_first.shape[2] + 1
    moves_in = MOVE_CAP * peers
    vmem = pl.BlockSpec(memory_space=pltpu.VMEM)
    places = [
        pltpu.VMEM((1, 3, blocks, width), F32),
        pltpu.VMEM((1, 3, blocks, width), F32),
        pltpu.VMEM(masses.shape, F32),
        pltpu.SMEM(counts.shape, jnp.int32),
        pltpu.SMEM((sources - 1, 1, blocks), jnp.int32),
        pltpu.SMEM(sends_first.shape, jnp.int32),
        pltpu.SMEM(new_slot.shape, jnp.int32),
        pltpu.VMEM(new_slot.shape, jnp.int32),
        pltpu.SMEM((sources - 1, 1, blocks), jnp.int32),
        pltpu.SMEM(sends_second.shape, jnp.int32),
        pltpu.SemaphoreType.DMA((10,)),
    ]
    scratch = places + [
        pltpu.VMEM((blocks, 8, width), F32),
        pltpu.VMEM((blocks, 8, width), F32),
        pltpu.VMEM((2 * halo, 8, width), F32),
        pltpu.VMEM((2 * halo, 8, width), F32),
        pltpu.VMEM((blocks, 8, width), F32),
        pltpu.VMEM((blocks + MOVE_CAP * peers, 8, width), F32),
        pltpu.VMEM((2 * halo, 8, width), F32),
        pltpu.VMEM((2 * halo, 8, width), F32),
        pltpu.VMEM((peers, MOVE_CAP, 8, width), F32),
        pltpu.VMEM((whole, 1, width), F32),
        pltpu.VMEM((whole, 1, width), F32),
        pltpu.VMEM((2 * halo, 1, width), F32),
        pltpu.VMEM((2 * halo, 1, width), F32),
        pltpu.VMEM((whole + moves_in, width, width), BF16),
        pltpu.VMEM((whole, 48, width), BF16),
        pltpu.VMEM((blocks + moves_in, width, 2 * width), BF16),
        pltpu.VMEM((whole, width, width), F32),
        pltpu.VMEM((whole + moves_in, width, width), F32),
        pltpu.VMEM((blocks, sources * width, width), BF16),
        pltpu.VMEM((blocks, sources * width, width), F32),
        pltpu.VMEM((1, width), jnp.int32),
        pltpu.VMEM((peers, 1, width), jnp.int32),
        pltpu.VMEM((whole, width), jnp.int32),
        pltpu.SMEM((whole, width), jnp.int32),
        pltpu.SemaphoreType.DMA((8,)),
        pltpu.SemaphoreType.DMA((8,)),
        pltpu.SemaphoreType.DMA((2 * peers,)),
        pltpu.SemaphoreType.DMA((2 * peers,)),
        pltpu.SemaphoreType.DMA,
    ]
    turned = jax.ShapeDtypeStruct((1, 3, blocks, width), F32)
    positions_out, velocities_out, densities_out = pl.pallas_call(
        functools.partial(kernel, n_curve, n_group),
        out_shape=(
            turned,
            turned,
            jax.ShapeDtypeStruct(masses.shape, F32),
        ),
        in_specs=[pl.BlockSpec(memory_space=pl.ANY)] * 9,
        out_specs=(vmem, vmem, vmem),
        scratch_shapes=scratch,
        compiler_params=pltpu.CompilerParams(
            collective_id=0, has_side_effects=True, vmem_limit_bytes=56 * 1024 * 1024
        ),
        name="sph",
    )(
        positions.transpose(0, 2, 1, 3), velocities.transpose(0, 2, 1, 3), masses, counts,
        neighbours_first.transpose(2, 0, 1), sends_first, new_slot,
        neighbours_second.transpose(2, 0, 1), sends_second,
    )
    return (
        positions_out.transpose(0, 2, 1, 3), velocities_out.transpose(0, 2, 1, 3), densities_out,
    )


def solution(mesh):
    blocks4 = P("group", "curve", None, None)
    blocks3 = P("group", "curve", None)
    blocks2 = P("group", "curve")
    in_specs = (
        blocks4, blocks4, blocks3, blocks2, blocks3, blocks2, blocks2, blocks3, blocks2,
    )
    return jax.shard_map(
        functools.partial(body, mesh.shape["curve"], mesh.shape["group"]),
        mesh=mesh, in_specs=in_specs, out_specs=(blocks4, blocks4, blocks3), check_vma=False,
    )
```

```python
import functools
import math

import jax
import jax.numpy as jnp
from jax import lax
from jax.experimental import pallas as pl
from jax.experimental.pallas import tpu as pltpu
from jax.sharding import PartitionSpec as P

KERNEL_SCALE = 4.0
SOFTENING = 0.0025
BACKGROUND = 0.5
TIME_STEP = 0.1
SPACING = 0.6
MOVE_CAP = 2
VMEM_BYTES = 56 * 1024 * 1024
SCALE = -KERNEL_SCALE
MESH = pl.DeviceIdType.MESH
F32 = jnp.float32
BF16 = jnp.bfloat16


def split(value):
    high = value.astype(BF16).astype(F32)
    rest = value - high
    middle = rest.astype(BF16).astype(F32)
    return high, middle, rest - middle


def source_rows(value):
    high, middle, low = split(value)
    return [high, middle, low, high, high, middle]


def target_rows(value):
    high, middle, low = split(value)
    return [high, high, high, middle, low, middle]


def rows_of(shape):
    return lax.broadcasted_iota(jnp.int32, shape, 0)


def moments(state, corner):
    row = rows_of(state.shape)
    state = state - jnp.where(row == 0, corner + 0.5, jnp.where(row < 3, 0.5, 0.0))
    square = jnp.sum(jnp.where(row < 3, state * state, 0.0), axis=0, keepdims=True)
    after = pltpu.roll(state, 3, 0)
    cross = jnp.sum(
        jnp.where((row >= 3) & (row < 6), state * after, 0.0), axis=0, keepdims=True
    )
    return row, state, after, square, cross


def prepare_source(state, corner, source_t):
    row, state, after, square, cross = moments(state, corner)
    lower = jnp.where(row < 6, state, jnp.where(row == 6, 1.0, square))
    upper = jnp.where(row == 0, cross, 0.0)
    pieces = source_rows(jnp.concatenate([lower, upper], axis=0))
    width = state.shape[1]
    used = len(pieces) * 2 * state.shape[0]
    pieces.append(jnp.zeros((width - used, width), F32))
    source_t[...] = jnp.concatenate(pieces, axis=0).astype(BF16).T


def prepare_target(state, corner, target):
    row, state, after, square, cross = moments(state, corner)
    width = state.shape[1]
    ahead = pltpu.roll(state, state.shape[0] - 3, 0)
    soft = jnp.where(
        row < 3,
        (-2.0 * SCALE) * state,
        jnp.where(
            row == 6, SCALE * (square + SOFTENING), jnp.where(row == 7, SCALE, 0.0)
        ),
    )
    closing = jnp.where(
        row < 3,
        -SCALE * ahead,
        jnp.where(row < 6, -SCALE * after, jnp.where(row == 6, SCALE * cross, 0.0)),
    )
    upper = jnp.where(row == 0, SCALE, 0.0)

    def table(low, high):
        pieces = target_rows(jnp.concatenate([low, high], axis=0))
        used = len(pieces) * 2 * low.shape[0]
        pieces.append(jnp.zeros((width - used, width), F32))
        return jnp.concatenate(pieces, axis=0).astype(BF16)

    target[:, 0:width] = table(soft, jnp.zeros_like(upper))
    target[:, width : 2 * width] = table(closing, upper)


def prepare_weights(state, corner, rho, source_m):
    row = rows_of(state.shape)
    mass = state[6:7]
    centred = state - jnp.where(row == 0, corner + 0.5, jnp.where(row < 3, 0.5, 0.0))
    weighted = jnp.where(row < 3, centred, jnp.where(row == 6, 1.0, 0.0)) * mass
    both = jnp.concatenate([weighted, weighted * (1.0 / rho)], axis=0)
    source_m[...] = jnp.concatenate(list(split(both)), axis=0).astype(BF16)


def gather(block, nbr, table, axis, place):
    picks = [block] + [nbr[item, 0, block] for item in range(nbr.shape[0])]
    picks = [place(pick) for pick in picks]
    return picks, jnp.concatenate([table[pick] for pick in picks], axis=axis)


LIFT = math.exp(KERNEL_SCALE * SOFTENING)


def own_density(block, nbr, source_t, target, mass_col, weights, drags, place):
    width = mass_col.shape[-1]
    picks, sources = gather(block, nbr, source_t, 0, place)
    both = jnp.dot(sources, target[place(block)], preferred_element_type=F32)
    total = None
    for item, pick in enumerate(picks):
        span = slice(item * width, (item + 1) * width)
        soft = both[span, 0:width]
        closing = jnp.maximum(both[span, width : 2 * width], 0.0)
        weight = jnp.exp(soft)
        term = weight * mass_col[pick]
        total = term if total is None else total + term
        weights[block, span, :] = weight.astype(BF16)
        drags[block, span, :] = weight * (closing * pl.reciprocal(soft, approx=True))
    return BACKGROUND + LIFT * jnp.sum(total, axis=0, keepdims=True)


def force_of(block, nbr, state, corner, rho, rho_col, source_m, weights, drags):
    width = state.shape[1]
    picks, weighted = gather(block, nbr, source_m, 1, lambda pick: pick)
    parts = []
    for item, pick in enumerate(picks):
        drag = drags[block, item * width : (item + 1) * width, :]
        parts.append((drag * pl.reciprocal(rho_col[pick] + rho, approx=True)).astype(BF16))
    right = jnp.concatenate([weights[block], jnp.concatenate(parts, axis=0)], axis=1)
    total = jnp.dot(weighted, right, preferred_element_type=F32)
    rows = state.shape[0]
    total = total[0 : 2 * rows] + total[2 * rows : 4 * rows] + total[4 * rows : 6 * rows]
    sums = (
        total[0:rows, 0:width] * (1.0 / rho)
        + total[rows : 2 * rows, 0:width]
        - total[0:rows, width : 2 * width]
    )
    row = rows_of(state.shape)
    centred = state - jnp.where(row == 0, corner + 0.5, jnp.where(row < 3, 0.5, 0.0))
    accel = (2.0 * KERNEL_SCALE * LIFT) * (centred * sums[6:7] - sums)
    velocity = state + TIME_STEP * pltpu.roll(accel, 3, 0)
    position = state + TIME_STEP * pltpu.roll(velocity, rows - 3, 0)
    return jnp.where(row < 3, position, jnp.where(row < 6, velocity, state))


def columns(rows, start, col):
    count, width = len(rows), rows[0].shape[1]
    rows = jnp.concatenate(rows, axis=0)
    turned = jnp.concatenate([rows, jnp.zeros((width - count, width), F32)], axis=0).T
    for item in range(count):
        col[start + item] = jnp.broadcast_to(turned[:, item : item + 1], (width, width))


def kernel(
    n_curve, n_group,
    pos_h, vel_h, mass_h, counts_h, nbr1_h, sends1_h, slots_h, nbr2_h, sends2_h,
    pos_out, vel_out, rho_out,
    pos, vel, mass, counts, nbr1, sends1, slots_s, slots_v, nbr2, sends2, in_sem,
    table1, table2, land1, land2, kept, moved, out1, out2, out_m, rho1, rho2, rho_i1, rho_i2, rho_s1, rho_s2,
    source_t, source_m, target, rho_col, mass_col, weights, drags,
    slots_own, slots_in, code_v, code_s,
    send_sem, recv_sem, send_g, recv_g, code_sem,
):
    blocks = pos.shape[2]
    width = pos.shape[3]
    halo = sends1.shape[1] // 2
    mine = lax.axis_index("curve")
    group = lax.axis_index("group")
    lower = lax.rem(mine + n_curve - 1, n_curve)
    upper = lax.rem(mine + 1, n_curve)
    corner = SPACING * mine.astype(F32)
    barrier = pltpu.get_barrier_semaphore()
    for other in (lower, upper):
        pl.semaphore_signal(barrier, inc=1, device_id={"curve": other}, device_id_type=MESH)
    peers = [lax.rem(group + step, n_group) for step in range(1, n_group)]
    for other in peers:
        pl.semaphore_signal(barrier, inc=1, device_id={"group": other}, device_id_type=MESH)

    loads = [
        pltpu.make_async_copy(source, landing, in_sem.at[item])
        for item, (source, landing) in enumerate(
            (
                (pos_h, pos), (vel_h, vel), (mass_h, mass), (counts_h, counts),
                (sends1_h, sends1), (slots_h, slots_v), (slots_h, slots_s),
                (nbr1_h, nbr1), (nbr2_h, nbr2), (sends2_h, sends2),
            )
        )
    ]
    for load in loads:
        load.start()
    lane = lax.broadcasted_iota(jnp.int32, (1, width), 1)
    for load in loads:
        load.wait()

    def load_state(block, carry):
        for axis in range(3):
            table1[block, axis : axis + 1, :] = pos[0, axis, pl.ds(block, 1), :]
            table1[block, 3 + axis : 4 + axis, :] = vel[0, axis, pl.ds(block, 1), :]
        live = jnp.where(lane < counts[0, block], mass[0, pl.ds(block, 1), :], 0.0)
        table1[block, 6:7, :] = live
        table1[block, 7:8, :] = jnp.zeros_like(live)
        return carry

    lax.fori_loop(0, blocks, load_state, 0, unroll=True)
    slots_own[...] = jnp.full(slots_own.shape, -1, jnp.int32)
    slots_own[:, 0:blocks] = slots_v[...]
    for item in range(2 * halo):
        out1[item] = table1[sends1[0, item]]
    pl.semaphore_wait(barrier, 2 + n_group - 1)

    def exchange(outgoing, landing, start, base):
        copies = []
        for side, other in ((0, lower), (1, upper)):
            copies.append(
                pltpu.make_async_remote_copy(
                    src_ref=outgoing.at[pl.ds(side * halo, halo)],
                    dst_ref=landing.at[pl.ds(start + (1 - side) * halo, halo)],
                    send_sem=send_sem.at[base + side],
                    recv_sem=recv_sem.at[base + side],
                    device_id={"curve": other},
                    device_id_type=MESH,
                )
            )
        for copy in copies:
            copy.start()
        return copies

    def finish(copies):
        for copy in copies:
            copy.wait()

    first = exchange(out1, land1, 0, 0)
    lists = []
    for step, other in enumerate(peers):
        copy = pltpu.make_async_remote_copy(
            src_ref=slots_own,
            dst_ref=slots_in.at[step],
            send_sem=send_g.at[step],
            recv_sem=recv_g.at[step],
            device_id={"group": other},
            device_id_type=MESH,
        )
        copy.start()
        lists.append(copy)

    def prepare(table, start, count, offset):
        def run(item, carry):
            state = table[start + item]
            prepare_source(state, corner, source_t.at[offset + item])
            prepare_target(state, corner, target.at[offset + item])
            return carry

        lax.fori_loop(0, count, run, 0, unroll=8)
        rows = [table[start + item, 6:7, :] for item in range(count)]
        columns(rows, offset, mass_col)

    def prepare_halo(land, offset):
        def run(item, carry):
            prepare_source(land[item], corner, source_t.at[offset + item])
            return carry

        lax.fori_loop(0, 2 * halo, run, 0, unroll=8)
        columns([land[item, 6:7, :] for item in range(2 * halo)], offset, mass_col)

    def sph(table, land, nbr, sends, rho, rho_in, rho_send, base, offset, place, write):
        prepare_halo(land, offset)

        def own(block, carry):
            rho[block] = own_density(
                block, nbr, source_t, target, mass_col, weights, drags, place
            )
            return carry

        lax.fori_loop(0, blocks, own, 0, unroll=2)
        for item in range(2 * halo):
            rho_send[item] = rho[sends[0, item]]
        copies = exchange(rho_send, rho_in, 0, base)

        def weigh(block, carry):
            prepare_weights(table[block], corner, rho[block], source_m.at[block])
            return carry

        lax.fori_loop(0, blocks, weigh, 0, unroll=4)
        columns([rho[block] for block in range(blocks)], 0, rho_col)
        finish(copies)
        columns([rho_in[item] for item in range(2 * halo)], blocks, rho_col)

        def weigh_halo(item, carry):
            prepare_weights(land[item], corner, rho_in[item], source_m.at[blocks + item])
            return carry

        lax.fori_loop(0, 2 * halo, weigh_halo, 0, unroll=4)

        def push(block, carry):
            write(
                block,
                force_of(
                    block, nbr, table[block], corner, rho[block],
                    rho_col, source_m, weights, drags,
                ),
            )
            return carry

        lax.fori_loop(0, blocks, push, 0, unroll=2)

    prepare(table1, 0, blocks, 0)
    finish(lists)
    wanted = rows_of((blocks, width)) + group * blocks
    lanes = lax.broadcasted_iota(jnp.int32, (blocks, width), 1)
    code = jnp.sum(jnp.where(slots_own[...] == wanted, lanes, 0), axis=1, keepdims=True)
    for step in range(n_group - 1):
        arrived = slots_in[step]
        here = (arrived >= group * blocks) & (arrived < (group + 1) * blocks)
        lead = jnp.min(jnp.where(here, lane, width), axis=1, keepdims=True)
        place = blocks + MOVE_CAP * step + jnp.where(lane > lead, 1, 0)
        code = code + jnp.sum(jnp.where(arrived == wanted, place, 0), axis=1, keepdims=True)
    code = jnp.minimum(code, moved.shape[0] - 1)
    code_v[0:blocks, :] = jnp.broadcast_to(code, (blocks, width))
    code_v[blocks:, :] = moved.shape[0] + rows_of((2 * halo, width))
    code_copy = pltpu.make_async_copy(code_v, code_s, code_sem)
    code_copy.start()
    finish(first)

    def keep(block, state):
        kept[block] = state

    sph(table1, land1, nbr1, sends1, rho1, rho_i1, rho_s1, 2, blocks, lambda pick: pick, keep)

    moves_in = MOVE_CAP * (n_group - 1)
    moves = []
    for step, other in enumerate(peers):
        one = jnp.int32(0)
        two = jnp.int32(0)
        for block in reversed(range(blocks)):
            owner = slots_s[0, block]
            goes = (owner >= other * blocks) & (owner < (other + 1) * blocks)
            two = jnp.where(goes, one, two)
            one = jnp.where(goes, block, one)
        out_m[step, 0] = kept[one]
        out_m[step, 1] = kept[two]
        copy = pltpu.make_async_remote_copy(
            src_ref=out_m.at[step],
            dst_ref=moved.at[pl.ds(blocks + MOVE_CAP * step, MOVE_CAP)],
            send_sem=send_g.at[n_group - 1 + step],
            recv_sem=recv_g.at[n_group - 1 + step],
            device_id={"group": other},
            device_id_type=MESH,
        )
        copy.start()
        moves.append(copy)
    code_copy.wait()
    for block in range(blocks):
        moved[block] = kept[block]
    prepare(kept, 0, blocks, 0)
    finish(moves)
    for item in range(2 * halo):
        out2[item] = moved[code_s[sends2[0, item], 0]]
    second = exchange(out2, land2, 0, 4)
    for block in range(blocks):
        table2[block] = moved[code_s[block, 0]]
    prepare(moved, blocks, moves_in, blocks)
    finish(second)

    def emit(block, state):
        for axis in range(3):
            pos_out[0, axis, pl.ds(block, 1), :] = state[axis : axis + 1]
            vel_out[0, axis, pl.ds(block, 1), :] = state[3 + axis : 4 + axis]
        rho_out[0, pl.ds(block, 1), :] = rho2[block]

    sph(
        table2, land2, nbr2, sends2, rho2, rho_i2, rho_s2, 6, blocks + moves_in,
        lambda pick: code_s[pick, 0], emit,
    )


def hand_over(first, second, third, first_out, second_out, third_out, sem):
    pairs = ((first, first_out), (second, second_out), (third, third_out))
    copies = [
        pltpu.make_async_copy(source, landing, sem.at[item])
        for item, (source, landing) in enumerate(pairs)
    ]
    for copy in copies:
        copy.start()
    for copy in copies:
        copy.wait()


def body(
    n_curve, n_group,
    positions, velocities, masses, counts, neighbours_first, sends_first, new_slot,
    neighbours_second, sends_second,
):
    blocks, width = masses.shape[1], masses.shape[2]
    halo = sends_first.shape[1] // 2
    whole = blocks + 2 * halo
    peers = n_group - 1
    sources = neighbours_first.shape[2] + 1
    moves_in = MOVE_CAP * peers
    vmem = pl.BlockSpec(memory_space=pltpu.VMEM)
    places = [
        pltpu.VMEM((1, 3, blocks, width), F32),
        pltpu.VMEM((1, 3, blocks, width), F32),
        pltpu.VMEM(masses.shape, F32),
        pltpu.SMEM(counts.shape, jnp.int32),
        pltpu.SMEM((sources - 1, 1, blocks), jnp.int32),
        pltpu.SMEM(sends_first.shape, jnp.int32),
        pltpu.SMEM(new_slot.shape, jnp.int32),
        pltpu.VMEM(new_slot.shape, jnp.int32),
        pltpu.SMEM((sources - 1, 1, blocks), jnp.int32),
        pltpu.SMEM(sends_second.shape, jnp.int32),
        pltpu.SemaphoreType.DMA((10,)),
    ]
    scratch = places + [
        pltpu.VMEM((blocks, 8, width), F32),
        pltpu.VMEM((blocks, 8, width), F32),
        pltpu.VMEM((2 * halo, 8, width), F32),
        pltpu.VMEM((2 * halo, 8, width), F32),
        pltpu.VMEM((blocks, 8, width), F32),
        pltpu.VMEM((blocks + MOVE_CAP * peers, 8, width), F32),
        pltpu.VMEM((2 * halo, 8, width), F32),
        pltpu.VMEM((2 * halo, 8, width), F32),
        pltpu.VMEM((peers, MOVE_CAP, 8, width), F32),
        pltpu.VMEM((blocks, 1, width), F32),
        pltpu.VMEM((blocks, 1, width), F32),
        pltpu.VMEM((2 * halo, 1, width), F32),
        pltpu.VMEM((2 * halo, 1, width), F32),
        pltpu.VMEM((2 * halo, 1, width), F32),
        pltpu.VMEM((2 * halo, 1, width), F32),
        pltpu.VMEM((whole + moves_in, width, width), BF16),
        pltpu.VMEM((whole, 48, width), BF16),
        pltpu.VMEM((blocks + moves_in, width, 2 * width), BF16),
        pltpu.VMEM((whole, width, width), F32),
        pltpu.VMEM((whole + moves_in, width, width), F32),
        pltpu.VMEM((blocks, sources * width, width), BF16),
        pltpu.VMEM((blocks, sources * width, width), F32),
        pltpu.VMEM((1, width), jnp.int32),
        pltpu.VMEM((peers, 1, width), jnp.int32),
        pltpu.VMEM((whole, width), jnp.int32),
        pltpu.SMEM((whole, width), jnp.int32),
        pltpu.SemaphoreType.DMA((8,)),
        pltpu.SemaphoreType.DMA((8,)),
        pltpu.SemaphoreType.DMA((2 * peers,)),
        pltpu.SemaphoreType.DMA((2 * peers,)),
        pltpu.SemaphoreType.DMA,
    ]
    turned = jax.ShapeDtypeStruct((1, 3, blocks, width), F32)
    positions_out, velocities_out, densities_out = pl.pallas_call(
        functools.partial(kernel, n_curve, n_group),
        out_shape=(
            turned,
            turned,
            jax.ShapeDtypeStruct(masses.shape, F32),
        ),
        in_specs=[pl.BlockSpec(memory_space=pl.ANY)] * 9,
        out_specs=(vmem, vmem, vmem),
        scratch_shapes=scratch,
        compiler_params=pltpu.CompilerParams(
            collective_id=0, has_side_effects=True, vmem_limit_bytes=VMEM_BYTES
        ),
        name="sph",
    )(
        positions.transpose(0, 2, 1, 3), velocities.transpose(0, 2, 1, 3), masses, counts,
        neighbours_first.transpose(2, 0, 1), sends_first, new_slot,
        neighbours_second.transpose(2, 0, 1), sends_second,
    )
    any_space = pl.BlockSpec(memory_space=pl.ANY)
    shapes = (turned, turned, jax.ShapeDtypeStruct(masses.shape, F32))
    positions_out, velocities_out, densities_out = pl.pallas_call(
        hand_over,
        out_shape=shapes,
        in_specs=[any_space] * 3,
        out_specs=(any_space,) * 3,
        scratch_shapes=[pltpu.SemaphoreType.DMA((3,))],
        compiler_params=pltpu.CompilerParams(vmem_limit_bytes=VMEM_BYTES),
        name="hand_over",
    )(positions_out, velocities_out, densities_out)
    return (
        positions_out.transpose(0, 2, 1, 3), velocities_out.transpose(0, 2, 1, 3), densities_out,
    )


def solution(mesh):
    blocks4 = P("group", "curve", None, None)
    blocks3 = P("group", "curve", None)
    blocks2 = P("group", "curve")
    in_specs = (
        blocks4, blocks4, blocks3, blocks2, blocks3, blocks2, blocks2, blocks3, blocks2,
    )
    return jax.shard_map(
        functools.partial(body, mesh.shape["curve"], mesh.shape["group"]),
        mesh=mesh, in_specs=in_specs, out_specs=(blocks4, blocks4, blocks3), check_vma=False,
    )
```

```python
import functools
import math

import jax
import jax.numpy as jnp
from jax import lax
from jax.experimental import pallas as pl
from jax.experimental.pallas import tpu as pltpu
from jax.sharding import PartitionSpec as P

KERNEL_SCALE = 4.0
SOFTENING = 0.0025
BACKGROUND = 0.5
TIME_STEP = 0.1
SPACING = 0.6
MOVE_CAP = 2
SCALE = -KERNEL_SCALE
MESH = pl.DeviceIdType.MESH
F32 = jnp.float32
BF16 = jnp.bfloat16


def split(value):
    high = value.astype(BF16).astype(F32)
    rest = value - high
    middle = rest.astype(BF16).astype(F32)
    return high, middle, rest - middle


def source_rows(value):
    high, middle, low = split(value)
    return [high, middle, low, high, high, middle]


def target_rows(value):
    high, middle, low = split(value)
    return [high, high, high, middle, low, middle]


def rows_of(shape):
    return lax.broadcasted_iota(jnp.int32, shape, 0)


def moments(state, corner):
    row = rows_of(state.shape)
    state = state - jnp.where(row == 0, corner + 0.5, jnp.where(row < 3, 0.5, 0.0))
    square = jnp.sum(jnp.where(row < 3, state * state, 0.0), axis=0, keepdims=True)
    after = pltpu.roll(state, 3, 0)
    cross = jnp.sum(
        jnp.where((row >= 3) & (row < 6), state * after, 0.0), axis=0, keepdims=True
    )
    return row, state, after, square, cross


def prepare_source(state, corner, source_t):
    row, state, after, square, cross = moments(state, corner)
    lower = jnp.where(row < 6, state, jnp.where(row == 6, 1.0, square))
    upper = jnp.where(row == 0, cross, 0.0)
    pieces = source_rows(jnp.concatenate([lower, upper], axis=0))
    width = state.shape[1]
    used = len(pieces) * 2 * state.shape[0]
    pieces.append(jnp.zeros((width - used, width), F32))
    source_t[...] = jnp.concatenate(pieces, axis=0).astype(BF16).T


def prepare_target(state, corner, target):
    row, state, after, square, cross = moments(state, corner)
    width = state.shape[1]
    ahead = pltpu.roll(state, state.shape[0] - 3, 0)
    soft = jnp.where(
        row < 3,
        (-2.0 * SCALE) * state,
        jnp.where(
            row == 6, SCALE * (square + SOFTENING), jnp.where(row == 7, SCALE, 0.0)
        ),
    )
    closing = jnp.where(
        row < 3,
        -SCALE * ahead,
        jnp.where(row < 6, -SCALE * after, jnp.where(row == 6, SCALE * cross, 0.0)),
    )
    upper = jnp.where(row == 0, SCALE, 0.0)

    def table(low, high):
        pieces = target_rows(jnp.concatenate([low, high], axis=0))
        used = len(pieces) * 2 * low.shape[0]
        pieces.append(jnp.zeros((width - used, width), F32))
        return jnp.concatenate(pieces, axis=0).astype(BF16)

    target[:, 0:width] = table(soft, jnp.zeros_like(upper))
    target[:, width : 2 * width] = table(closing, upper)


def prepare_weights(state, corner, rho, source_m):
    row = rows_of(state.shape)
    mass = state[6:7]
    centred = state - jnp.where(row == 0, corner + 0.5, jnp.where(row < 3, 0.5, 0.0))
    weighted = jnp.where(row < 3, centred, jnp.where(row == 6, 1.0, 0.0)) * mass
    both = jnp.concatenate([weighted, weighted * (1.0 / rho)], axis=0)
    source_m[...] = jnp.concatenate(list(split(both)), axis=0).astype(BF16)


def gather(block, nbr, table, axis, place):
    picks = [block] + [nbr[item, 0, block] for item in range(nbr.shape[0])]
    picks = [place(pick) for pick in picks]
    return picks, jnp.concatenate([table[pick] for pick in picks], axis=axis)


LIFT = math.exp(KERNEL_SCALE * SOFTENING)


def listed_density(block, nbr, source_t, target, mass_col, place):
    width = mass_col.shape[-1]
    picks, sources = gather(block, nbr, source_t, 0, place)
    soft = jnp.dot(sources, target[place(block), :, 0:width], preferred_element_type=F32)
    total = None
    for item, pick in enumerate(picks):
        term = jnp.exp(soft[item * width : (item + 1) * width]) * mass_col[pick]
        total = term if total is None else total + term
    return BACKGROUND + LIFT * jnp.sum(total, axis=0, keepdims=True)


def own_density(block, nbr, source_t, target, mass_col, weights, drags, place):
    width = mass_col.shape[-1]
    picks, sources = gather(block, nbr, source_t, 0, place)
    both = jnp.dot(sources, target[place(block)], preferred_element_type=F32)
    total = None
    for item, pick in enumerate(picks):
        span = slice(item * width, (item + 1) * width)
        soft = both[span, 0:width]
        closing = jnp.maximum(both[span, width : 2 * width], 0.0)
        weight = jnp.exp(soft)
        term = weight * mass_col[pick]
        total = term if total is None else total + term
        weights[block, span, :] = weight.astype(BF16)
        drags[block, span, :] = weight * (closing * pl.reciprocal(soft, approx=True))
    return BACKGROUND + LIFT * jnp.sum(total, axis=0, keepdims=True)


def force_of(block, nbr, state, corner, rho, rho_col, source_m, weights, drags):
    width = state.shape[1]
    picks, weighted = gather(block, nbr, source_m, 1, lambda pick: pick)
    parts = []
    for item, pick in enumerate(picks):
        drag = drags[block, item * width : (item + 1) * width, :]
        parts.append((drag * pl.reciprocal(rho_col[pick] + rho, approx=True)).astype(BF16))
    right = jnp.concatenate([weights[block], jnp.concatenate(parts, axis=0)], axis=1)
    total = jnp.dot(weighted, right, preferred_element_type=F32)
    rows = state.shape[0]
    total = total[0 : 2 * rows] + total[2 * rows : 4 * rows] + total[4 * rows : 6 * rows]
    sums = (
        total[0:rows, 0:width] * (1.0 / rho)
        + total[rows : 2 * rows, 0:width]
        - total[0:rows, width : 2 * width]
    )
    row = rows_of(state.shape)
    centred = state - jnp.where(row == 0, corner + 0.5, jnp.where(row < 3, 0.5, 0.0))
    accel = (2.0 * KERNEL_SCALE * LIFT) * (centred * sums[6:7] - sums)
    velocity = state + TIME_STEP * pltpu.roll(accel, 3, 0)
    position = state + TIME_STEP * pltpu.roll(velocity, rows - 3, 0)
    return jnp.where(row < 3, position, jnp.where(row < 6, velocity, state))


def columns(rows, start, col):
    count, width = len(rows), rows[0].shape[1]
    rows = jnp.concatenate(rows, axis=0)
    turned = jnp.concatenate([rows, jnp.zeros((width - count, width), F32)], axis=0).T
    for item in range(count):
        col[start + item] = jnp.broadcast_to(turned[:, item : item + 1], (width, width))


def kernel(
    n_curve, n_group,
    pos_h, vel_h, mass_h, counts_h, nbr1_h, sends1_h, slots_h, nbr2_h, sends2_h,
    pos_out, vel_out, rho_out,
    pos, vel, mass, counts, nbr1, sends1, slots_s, slots_v, nbr2, sends2, in_sem,
    table1, table2, land1, land2, kept, moved, out1, out2, out_m, rho1, rho2, rho_s1, rho_s2,
    source_t, source_m, target, rho_col, mass_col, weights, drags,
    slots_own, slots_in, code_v, code_s,
    send_sem, recv_sem, send_g, recv_g, code_sem,
):
    blocks = pos.shape[2]
    width = pos.shape[3]
    halo = sends1.shape[1] // 2
    mine = lax.axis_index("curve")
    group = lax.axis_index("group")
    lower = lax.rem(mine + n_curve - 1, n_curve)
    upper = lax.rem(mine + 1, n_curve)
    corner = SPACING * mine.astype(F32)
    barrier = pltpu.get_barrier_semaphore()
    for other in (lower, upper):
        pl.semaphore_signal(barrier, inc=1, device_id={"curve": other}, device_id_type=MESH)
    peers = [lax.rem(group + step, n_group) for step in range(1, n_group)]
    for other in peers:
        pl.semaphore_signal(barrier, inc=1, device_id={"group": other}, device_id_type=MESH)

    loads = [
        pltpu.make_async_copy(source, landing, in_sem.at[item])
        for item, (source, landing) in enumerate(
            (
                (pos_h, pos), (vel_h, vel), (mass_h, mass), (counts_h, counts),
                (sends1_h, sends1), (slots_h, slots_v), (slots_h, slots_s),
                (nbr1_h, nbr1), (nbr2_h, nbr2), (sends2_h, sends2),
            )
        )
    ]
    for load in loads:
        load.start()
    lane = lax.broadcasted_iota(jnp.int32, (1, width), 1)
    for load in loads:
        load.wait()

    def load_state(block, carry):
        for axis in range(3):
            table1[block, axis : axis + 1, :] = pos[0, axis, pl.ds(block, 1), :]
            table1[block, 3 + axis : 4 + axis, :] = vel[0, axis, pl.ds(block, 1), :]
        live = jnp.where(lane < counts[0, block], mass[0, pl.ds(block, 1), :], 0.0)
        table1[block, 6:7, :] = live
        table1[block, 7:8, :] = jnp.zeros_like(live)
        return carry

    lax.fori_loop(0, blocks, load_state, 0, unroll=True)
    slots_own[...] = jnp.full(slots_own.shape, -1, jnp.int32)
    slots_own[:, 0:blocks] = slots_v[...]
    for item in range(2 * halo):
        out1[item] = table1[sends1[0, item]]
    pl.semaphore_wait(barrier, 2 + n_group - 1)

    def exchange(outgoing, landing, start, base):
        copies = []
        for side, other in ((0, lower), (1, upper)):
            copies.append(
                pltpu.make_async_remote_copy(
                    src_ref=outgoing.at[pl.ds(side * halo, halo)],
                    dst_ref=landing.at[pl.ds(start + (1 - side) * halo, halo)],
                    send_sem=send_sem.at[base + side],
                    recv_sem=recv_sem.at[base + side],
                    device_id={"curve": other},
                    device_id_type=MESH,
                )
            )
        for copy in copies:
            copy.start()
        return copies

    def finish(copies):
        for copy in copies:
            copy.wait()

    first = exchange(out1, land1, 0, 0)
    lists = []
    for step, other in enumerate(peers):
        copy = pltpu.make_async_remote_copy(
            src_ref=slots_own,
            dst_ref=slots_in.at[step],
            send_sem=send_g.at[step],
            recv_sem=recv_g.at[step],
            device_id={"group": other},
            device_id_type=MESH,
        )
        copy.start()
        lists.append(copy)

    def prepare(table, start, count, offset):
        def run(item, carry):
            state = table[start + item]
            prepare_source(state, corner, source_t.at[offset + item])
            prepare_target(state, corner, target.at[offset + item])
            return carry

        lax.fori_loop(0, count, run, 0, unroll=8)
        rows = [table[start + item, 6:7, :] for item in range(count)]
        columns(rows, offset, mass_col)

    def prepare_halo(land, offset):
        def run(item, carry):
            prepare_source(land[item], corner, source_t.at[offset + item])
            return carry

        lax.fori_loop(0, 2 * halo, run, 0, unroll=8)
        columns([land[item, 6:7, :] for item in range(2 * halo)], offset, mass_col)

    def sph(table, land, nbr, sends, rho, rho_send, base, offset, place, ahead, write):
        prepare_halo(land, offset)

        def listed(item, carry):
            rho_send[item] = listed_density(
                sends[0, item], nbr, source_t, target, mass_col, place
            )
            return carry

        lax.fori_loop(0, 2 * halo, listed, 0, unroll=4)
        copies = exchange(rho_send, rho, blocks, base)

        def own(block, carry):
            rho[block] = own_density(
                block, nbr, source_t, target, mass_col, weights, drags, place
            )
            return carry

        lax.fori_loop(0, blocks, own, 0, unroll=2)
        def weigh(block, carry):
            prepare_weights(table[block], corner, rho[block], source_m.at[block])
            return carry

        lax.fori_loop(0, blocks, weigh, 0, unroll=4)
        columns([rho[block] for block in range(blocks)], 0, rho_col)
        finish(copies)
        columns([rho[blocks + item] for item in range(2 * halo)], blocks, rho_col)

        def weigh_halo(item, carry):
            block = blocks + item
            prepare_weights(land[item], corner, rho[block], source_m.at[block])
            return carry

        lax.fori_loop(0, 2 * halo, weigh_halo, 0, unroll=4)

        def pushed(block):
            return force_of(
                block, nbr, table[block], corner, rho[block],
                rho_col, source_m, weights, drags,
            )

        ahead(pushed)

        def push(block, carry):
            write(block, pushed(block))
            return carry

        lax.fori_loop(0, blocks, push, 0, unroll=2)

    prepare(table1, 0, blocks, 0)
    finish(lists)
    wanted = rows_of((blocks, width)) + group * blocks
    lanes = lax.broadcasted_iota(jnp.int32, (blocks, width), 1)
    code = jnp.sum(jnp.where(slots_own[...] == wanted, lanes, 0), axis=1, keepdims=True)
    for step in range(n_group - 1):
        arrived = slots_in[step]
        here = (arrived >= group * blocks) & (arrived < (group + 1) * blocks)
        lead = jnp.min(jnp.where(here, lane, width), axis=1, keepdims=True)
        place = blocks + MOVE_CAP * step + jnp.where(lane > lead, 1, 0)
        code = code + jnp.sum(jnp.where(arrived == wanted, place, 0), axis=1, keepdims=True)
    code = jnp.minimum(code, moved.shape[0] - 1)
    code_v[0:blocks, :] = jnp.broadcast_to(code, (blocks, width))
    code_v[blocks:, :] = moved.shape[0] + rows_of((2 * halo, width))
    code_copy = pltpu.make_async_copy(code_v, code_s, code_sem)
    code_copy.start()
    finish(first)

    def keep(block, state):
        kept[block] = state

    moves_in = MOVE_CAP * (n_group - 1)
    moves = []

    def send_moving(pushed):
        for step, other in enumerate(peers):
            one = jnp.int32(0)
            two = jnp.int32(0)
            for block in reversed(range(blocks)):
                owner = slots_s[0, block]
                goes = (owner >= other * blocks) & (owner < (other + 1) * blocks)
                two = jnp.where(goes, one, two)
                one = jnp.where(goes, block, one)
            out_m[step, 0] = pushed(one)
            out_m[step, 1] = pushed(two)
            copy = pltpu.make_async_remote_copy(
                src_ref=out_m.at[step],
                dst_ref=moved.at[pl.ds(blocks + MOVE_CAP * step, MOVE_CAP)],
                send_sem=send_g.at[n_group - 1 + step],
                recv_sem=recv_g.at[n_group - 1 + step],
                device_id={"group": other},
                device_id_type=MESH,
            )
            copy.start()
            moves.append(copy)

    sph(
        table1, land1, nbr1, sends1, rho1, rho_s1, 2, blocks, lambda pick: pick,
        send_moving, keep,
    )

    code_copy.wait()
    for block in range(blocks):
        moved[block] = kept[block]
    finish(moves)
    for item in range(2 * halo):
        out2[item] = moved[code_s[sends2[0, item], 0]]
    second = exchange(out2, land2, 0, 4)
    for block in range(blocks):
        table2[block] = moved[code_s[block, 0]]
    prepare(kept, 0, blocks, 0)
    prepare(moved, blocks, moves_in, blocks)
    finish(second)

    def emit(block, state):
        for axis in range(3):
            pos_out[0, axis, pl.ds(block, 1), :] = state[axis : axis + 1]
            vel_out[0, axis, pl.ds(block, 1), :] = state[3 + axis : 4 + axis]
        rho_out[0, pl.ds(block, 1), :] = rho2[block]

    sph(
        table2, land2, nbr2, sends2, rho2, rho_s2, 6, blocks + moves_in,
        lambda pick: code_s[pick, 0],
        lambda pushed: None, emit,
    )


def body(
    n_curve, n_group,
    positions, velocities, masses, counts, neighbours_first, sends_first, new_slot,
    neighbours_second, sends_second,
):
    blocks, width = masses.shape[1], masses.shape[2]
    halo = sends_first.shape[1] // 2
    whole = blocks + 2 * halo
    peers = n_group - 1
    sources = neighbours_first.shape[2] + 1
    moves_in = MOVE_CAP * peers
    vmem = pl.BlockSpec(memory_space=pltpu.VMEM)
    places = [
        pltpu.VMEM((1, 3, blocks, width), F32),
        pltpu.VMEM((1, 3, blocks, width), F32),
        pltpu.VMEM(masses.shape, F32),
        pltpu.SMEM(counts.shape, jnp.int32),
        pltpu.SMEM((sources - 1, 1, blocks), jnp.int32),
        pltpu.SMEM(sends_first.shape, jnp.int32),
        pltpu.SMEM(new_slot.shape, jnp.int32),
        pltpu.VMEM(new_slot.shape, jnp.int32),
        pltpu.SMEM((sources - 1, 1, blocks), jnp.int32),
        pltpu.SMEM(sends_second.shape, jnp.int32),
        pltpu.SemaphoreType.DMA((10,)),
    ]
    scratch = places + [
        pltpu.VMEM((blocks, 8, width), F32),
        pltpu.VMEM((blocks, 8, width), F32),
        pltpu.VMEM((2 * halo, 8, width), F32),
        pltpu.VMEM((2 * halo, 8, width), F32),
        pltpu.VMEM((blocks, 8, width), F32),
        pltpu.VMEM((blocks + MOVE_CAP * peers, 8, width), F32),
        pltpu.VMEM((2 * halo, 8, width), F32),
        pltpu.VMEM((2 * halo, 8, width), F32),
        pltpu.VMEM((peers, MOVE_CAP, 8, width), F32),
        pltpu.VMEM((whole, 1, width), F32),
        pltpu.VMEM((whole, 1, width), F32),
        pltpu.VMEM((2 * halo, 1, width), F32),
        pltpu.VMEM((2 * halo, 1, width), F32),
        pltpu.VMEM((whole + moves_in, width, width), BF16),
        pltpu.VMEM((whole, 48, width), BF16),
        pltpu.VMEM((blocks + moves_in, width, 2 * width), BF16),
        pltpu.VMEM((whole, width, width), F32),
        pltpu.VMEM((whole + moves_in, width, width), F32),
        pltpu.VMEM((blocks, sources * width, width), BF16),
        pltpu.VMEM((blocks, sources * width, width), F32),
        pltpu.VMEM((1, width), jnp.int32),
        pltpu.VMEM((peers, 1, width), jnp.int32),
        pltpu.VMEM((whole, width), jnp.int32),
        pltpu.SMEM((whole, width), jnp.int32),
        pltpu.SemaphoreType.DMA((8,)),
        pltpu.SemaphoreType.DMA((8,)),
        pltpu.SemaphoreType.DMA((2 * peers,)),
        pltpu.SemaphoreType.DMA((2 * peers,)),
        pltpu.SemaphoreType.DMA,
    ]
    turned = jax.ShapeDtypeStruct((1, 3, blocks, width), F32)
    positions_out, velocities_out, densities_out = pl.pallas_call(
        functools.partial(kernel, n_curve, n_group),
        out_shape=(
            turned,
            turned,
            jax.ShapeDtypeStruct(masses.shape, F32),
        ),
        in_specs=[pl.BlockSpec(memory_space=pl.ANY)] * 9,
        out_specs=(vmem, vmem, vmem),
        scratch_shapes=scratch,
        compiler_params=pltpu.CompilerParams(
            collective_id=0, has_side_effects=True, vmem_limit_bytes=56 * 1024 * 1024
        ),
        name="sph",
    )(
        positions.transpose(0, 2, 1, 3), velocities.transpose(0, 2, 1, 3), masses, counts,
        neighbours_first.transpose(2, 0, 1), sends_first, new_slot,
        neighbours_second.transpose(2, 0, 1), sends_second,
    )
    return (
        positions_out.transpose(0, 2, 1, 3), velocities_out.transpose(0, 2, 1, 3), densities_out,
    )


def solution(mesh):
    blocks4 = P("group", "curve", None, None)
    blocks3 = P("group", "curve", None)
    blocks2 = P("group", "curve")
    in_specs = (
        blocks4, blocks4, blocks3, blocks2, blocks3, blocks2, blocks2, blocks3, blocks2,
    )
    return jax.shard_map(
        functools.partial(body, mesh.shape["curve"], mesh.shape["group"]),
        mesh=mesh, in_specs=in_specs, out_specs=(blocks4, blocks4, blocks3), check_vma=False,
    )
```

```python
import functools
import math

import jax
import jax.numpy as jnp
from jax import lax
from jax.experimental import pallas as pl
from jax.experimental.pallas import tpu as pltpu
from jax.sharding import PartitionSpec as P

KERNEL_SCALE = 4.0
SOFTENING = 0.0025
BACKGROUND = 0.5
TIME_STEP = 0.1
SPACING = 0.6
MOVE_CAP = 2
SCALE = -KERNEL_SCALE
MESH = pl.DeviceIdType.MESH
F32 = jnp.float32
BF16 = jnp.bfloat16


def split(value):
    high = value.astype(BF16).astype(F32)
    rest = value - high
    middle = rest.astype(BF16).astype(F32)
    return high, middle, rest - middle


def source_rows(value):
    high, middle, low = split(value)
    return [high, middle, low, high, high, middle]


def target_rows(value):
    high, middle, low = split(value)
    return [high, high, high, middle, low, middle]


def rows_of(shape):
    return lax.broadcasted_iota(jnp.int32, shape, 0)


def moments(state, corner):
    row = rows_of(state.shape)
    state = state - jnp.where(row == 0, corner + 0.5, jnp.where(row < 3, 0.5, 0.0))
    square = jnp.sum(jnp.where(row < 3, state * state, 0.0), axis=0, keepdims=True)
    after = pltpu.roll(state, 3, 0)
    cross = jnp.sum(
        jnp.where((row >= 3) & (row < 6), state * after, 0.0), axis=0, keepdims=True
    )
    return row, state, after, square, cross


def prepare_source(state, corner, source_t):
    row, state, after, square, cross = moments(state, corner)
    lower = jnp.where(row < 6, state, jnp.where(row == 6, 1.0, square))
    upper = jnp.where(row == 0, cross, 0.0)
    pieces = source_rows(jnp.concatenate([lower, upper], axis=0))
    width = state.shape[1]
    used = len(pieces) * 2 * state.shape[0]
    pieces.append(jnp.zeros((width - used, width), F32))
    source_t[...] = jnp.concatenate(pieces, axis=0).astype(BF16).T


def prepare_target(state, corner, target):
    row, state, after, square, cross = moments(state, corner)
    width = state.shape[1]
    ahead = pltpu.roll(state, state.shape[0] - 3, 0)
    soft = jnp.where(
        row < 3,
        (-2.0 * SCALE) * state,
        jnp.where(
            row == 6, SCALE * (square + SOFTENING), jnp.where(row == 7, SCALE, 0.0)
        ),
    )
    closing = jnp.where(
        row < 3,
        -SCALE * ahead,
        jnp.where(row < 6, -SCALE * after, jnp.where(row == 6, SCALE * cross, 0.0)),
    )
    upper = jnp.where(row == 0, SCALE, 0.0)

    def table(low, high):
        pieces = target_rows(jnp.concatenate([low, high], axis=0))
        used = len(pieces) * 2 * low.shape[0]
        pieces.append(jnp.zeros((width - used, width), F32))
        return jnp.concatenate(pieces, axis=0).astype(BF16)

    target[:, 0:width] = table(soft, jnp.zeros_like(upper))
    target[:, width : 2 * width] = table(closing, upper)


def prepare_weights(state, corner, rho, source_m):
    row = rows_of(state.shape)
    mass = state[6:7]
    centred = state - jnp.where(row == 0, corner + 0.5, jnp.where(row < 3, 0.5, 0.0))
    weighted = jnp.where(row < 3, centred, jnp.where(row == 6, 1.0, 0.0)) * mass
    both = jnp.concatenate([weighted, weighted * (1.0 / rho)], axis=0)
    source_m[...] = jnp.concatenate(list(split(both)), axis=0).astype(BF16)


def gather(block, nbr, table, axis, place):
    picks = [block] + [nbr[item, 0, block] for item in range(nbr.shape[0])]
    picks = [place(pick) for pick in picks]
    return picks, jnp.concatenate([table[pick] for pick in picks], axis=axis)


LIFT = math.exp(KERNEL_SCALE * SOFTENING)


def listed_density(block, nbr, source_t, target, mass_col, place):
    width = mass_col.shape[-1]
    picks, sources = gather(block, nbr, source_t, 0, place)
    soft = jnp.dot(sources, target[place(block), :, 0:width], preferred_element_type=F32)
    total = None
    for item, pick in enumerate(picks):
        term = jnp.exp(soft[item * width : (item + 1) * width]) * mass_col[pick]
        total = term if total is None else total + term
    return BACKGROUND + LIFT * jnp.sum(total, axis=0, keepdims=True)


def own_density(block, nbr, source_t, target, mass_col, weights, drags, place):
    width = mass_col.shape[-1]
    picks, sources = gather(block, nbr, source_t, 0, place)
    both = jnp.dot(sources, target[place(block)], preferred_element_type=F32)
    total = None
    for item, pick in enumerate(picks):
        span = slice(item * width, (item + 1) * width)
        soft = both[span, 0:width]
        closing = jnp.maximum(both[span, width : 2 * width], 0.0)
        weight = jnp.exp(soft)
        term = weight * mass_col[pick]
        total = term if total is None else total + term
        weights[block, span, :] = weight.astype(BF16)
        drags[block, span, :] = weight * (closing * pl.reciprocal(soft, approx=True))
    return BACKGROUND + LIFT * jnp.sum(total, axis=0, keepdims=True)


def force_of(block, nbr, state, corner, rho, rho_col, source_m, weights, drags):
    width = state.shape[1]
    picks, weighted = gather(block, nbr, source_m, 1, lambda pick: pick)
    parts = []
    for item, pick in enumerate(picks):
        drag = drags[block, item * width : (item + 1) * width, :]
        parts.append((drag * pl.reciprocal(rho_col[pick] + rho, approx=True)).astype(BF16))
    right = jnp.concatenate([weights[block], jnp.concatenate(parts, axis=0)], axis=1)
    total = jnp.dot(weighted, right, preferred_element_type=F32)
    rows = state.shape[0]
    total = total[0 : 2 * rows] + total[2 * rows : 4 * rows] + total[4 * rows : 6 * rows]
    sums = (
        total[0:rows, 0:width] * (1.0 / rho)
        + total[rows : 2 * rows, 0:width]
        - total[0:rows, width : 2 * width]
    )
    row = rows_of(state.shape)
    centred = state - jnp.where(row == 0, corner + 0.5, jnp.where(row < 3, 0.5, 0.0))
    accel = (2.0 * KERNEL_SCALE * LIFT) * (centred * sums[6:7] - sums)
    velocity = state + TIME_STEP * pltpu.roll(accel, 3, 0)
    position = state + TIME_STEP * pltpu.roll(velocity, rows - 3, 0)
    return jnp.where(row < 3, position, jnp.where(row < 6, velocity, state))


def columns(rows, start, col):
    count, width = len(rows), rows[0].shape[1]
    rows = jnp.concatenate(rows, axis=0)
    turned = jnp.concatenate([rows, jnp.zeros((width - count, width), F32)], axis=0).T
    for item in range(count):
        col[start + item] = jnp.broadcast_to(turned[:, item : item + 1], (width, width))


def kernel(
    n_curve, n_group,
    pos_h, vel_h, mass_h, counts_h, nbr1_h, sends1_h, slots_h, nbr2_h, sends2_h,
    pos_out, vel_out, rho_out,
    pos, vel, mass, counts, nbr1, sends1, slots_s, slots_v, nbr2, sends2, in_sem,
    table1, table2, land1, land2, kept, moved, out1, out2, out_m, rho1, rho2, rho_s1, rho_s2,
    source_t, source_m, target, rho_col, mass_col, weights, drags,
    slots_own, slots_in, code_v, code_s,
    send_sem, recv_sem, send_g, recv_g, code_sem,
):
    blocks = pos.shape[2]
    width = pos.shape[3]
    halo = sends1.shape[1] // 2
    mine = lax.axis_index("curve")
    group = lax.axis_index("group")
    lower = lax.rem(mine + n_curve - 1, n_curve)
    upper = lax.rem(mine + 1, n_curve)
    corner = SPACING * mine.astype(F32)
    barrier = pltpu.get_barrier_semaphore()
    for other in (lower, upper):
        pl.semaphore_signal(barrier, inc=1, device_id={"curve": other}, device_id_type=MESH)
    peers = [lax.rem(group + step, n_group) for step in range(1, n_group)]
    for other in peers:
        pl.semaphore_signal(barrier, inc=1, device_id={"group": other}, device_id_type=MESH)

    loads = [
        pltpu.make_async_copy(source, landing, in_sem.at[item])
        for item, (source, landing) in enumerate(
            (
                (pos_h, pos), (vel_h, vel), (mass_h, mass), (counts_h, counts),
                (sends1_h, sends1), (slots_h, slots_v), (slots_h, slots_s),
                (nbr1_h, nbr1), (nbr2_h, nbr2), (sends2_h, sends2),
            )
        )
    ]
    for load in loads:
        load.start()
    lane = lax.broadcasted_iota(jnp.int32, (1, width), 1)
    for load in loads:
        load.wait()

    def load_state(block, carry):
        for axis in range(3):
            table1[block, axis : axis + 1, :] = pos[0, axis, pl.ds(block, 1), :]
            table1[block, 3 + axis : 4 + axis, :] = vel[0, axis, pl.ds(block, 1), :]
        live = jnp.where(lane < counts[0, block], mass[0, pl.ds(block, 1), :], 0.0)
        table1[block, 6:7, :] = live
        table1[block, 7:8, :] = jnp.zeros_like(live)
        return carry

    lax.fori_loop(0, blocks, load_state, 0, unroll=True)
    slots_own[...] = jnp.full(slots_own.shape, -1, jnp.int32)
    slots_own[:, 0:blocks] = slots_v[...]
    for item in range(2 * halo):
        out1[item] = table1[sends1[0, item]]
    pl.semaphore_wait(barrier, 2 + n_group - 1)

    def exchange(outgoing, landing, start, base):
        copies = []
        for side, other in ((0, lower), (1, upper)):
            copies.append(
                pltpu.make_async_remote_copy(
                    src_ref=outgoing.at[pl.ds(side * halo, halo)],
                    dst_ref=landing.at[pl.ds(start + (1 - side) * halo, halo)],
                    send_sem=send_sem.at[base + side],
                    recv_sem=recv_sem.at[base + side],
                    device_id={"curve": other},
                    device_id_type=MESH,
                )
            )
        for copy in copies:
            copy.start()
        return copies

    def finish(copies):
        for copy in copies:
            copy.wait()

    first = exchange(out1, land1, 0, 0)
    lists = []
    for step, other in enumerate(peers):
        copy = pltpu.make_async_remote_copy(
            src_ref=slots_own,
            dst_ref=slots_in.at[step],
            send_sem=send_g.at[step],
            recv_sem=recv_g.at[step],
            device_id={"group": other},
            device_id_type=MESH,
        )
        copy.start()
        lists.append(copy)

    def prepare(table, start, count, offset):
        def run(item, carry):
            state = table[start + item]
            prepare_source(state, corner, source_t.at[offset + item])
            prepare_target(state, corner, target.at[offset + item])
            return carry

        lax.fori_loop(0, count, run, 0, unroll=8)
        rows = [table[start + item, 6:7, :] for item in range(count)]
        columns(rows, offset, mass_col)

    def prepare_halo(land, offset):
        def run(item, carry):
            prepare_source(land[item], corner, source_t.at[offset + item])
            return carry

        lax.fori_loop(0, 2 * halo, run, 0, unroll=8)
        columns([land[item, 6:7, :] for item in range(2 * halo)], offset, mass_col)

    def sph(table, land, nbr, sends, rho, rho_send, base, offset, place, ahead, write):
        prepare_halo(land, offset)

        def listed(item, carry):
            rho_send[item] = listed_density(
                sends[0, item], nbr, source_t, target, mass_col, place
            )
            return carry

        lax.fori_loop(0, 2 * halo, listed, 0, unroll=8)
        copies = exchange(rho_send, rho, blocks, base)

        def own(block, carry):
            rho[block] = own_density(
                block, nbr, source_t, target, mass_col, weights, drags, place
            )
            return carry

        lax.fori_loop(0, blocks, own, 0, unroll=4)
        def weigh(block, carry):
            prepare_weights(table[block], corner, rho[block], source_m.at[block])
            return carry

        lax.fori_loop(0, blocks, weigh, 0, unroll=8)
        columns([rho[block] for block in range(blocks)], 0, rho_col)
        finish(copies)
        columns([rho[blocks + item] for item in range(2 * halo)], blocks, rho_col)

        def weigh_halo(item, carry):
            block = blocks + item
            prepare_weights(land[item], corner, rho[block], source_m.at[block])
            return carry

        lax.fori_loop(0, 2 * halo, weigh_halo, 0, unroll=8)

        def pushed(block):
            return force_of(
                block, nbr, table[block], corner, rho[block],
                rho_col, source_m, weights, drags,
            )

        ahead(pushed)

        def push(block, carry):
            write(block, pushed(block))
            return carry

        lax.fori_loop(0, blocks, push, 0, unroll=8)

    prepare(table1, 0, blocks, 0)
    finish(lists)
    wanted = rows_of((blocks, width)) + group * blocks
    lanes = lax.broadcasted_iota(jnp.int32, (blocks, width), 1)
    code = jnp.sum(jnp.where(slots_own[...] == wanted, lanes, 0), axis=1, keepdims=True)
    for step in range(n_group - 1):
        arrived = slots_in[step]
        here = (arrived >= group * blocks) & (arrived < (group + 1) * blocks)
        lead = jnp.min(jnp.where(here, lane, width), axis=1, keepdims=True)
        place = blocks + MOVE_CAP * step + jnp.where(lane > lead, 1, 0)
        code = code + jnp.sum(jnp.where(arrived == wanted, place, 0), axis=1, keepdims=True)
    code = jnp.minimum(code, moved.shape[0] - 1)
    code_v[0:blocks, :] = jnp.broadcast_to(code, (blocks, width))
    code_v[blocks:, :] = moved.shape[0] + rows_of((2 * halo, width))
    code_copy = pltpu.make_async_copy(code_v, code_s, code_sem)
    code_copy.start()
    finish(first)

    def keep(block, state):
        kept[block] = state

    moves_in = MOVE_CAP * (n_group - 1)
    moves = []

    def send_moving(pushed):
        for step, other in enumerate(peers):
            one = jnp.int32(0)
            two = jnp.int32(0)
            for block in reversed(range(blocks)):
                owner = slots_s[0, block]
                goes = (owner >= other * blocks) & (owner < (other + 1) * blocks)
                two = jnp.where(goes, one, two)
                one = jnp.where(goes, block, one)
            out_m[step, 0] = pushed(one)
            out_m[step, 1] = pushed(two)
            copy = pltpu.make_async_remote_copy(
                src_ref=out_m.at[step],
                dst_ref=moved.at[pl.ds(blocks + MOVE_CAP * step, MOVE_CAP)],
                send_sem=send_g.at[n_group - 1 + step],
                recv_sem=recv_g.at[n_group - 1 + step],
                device_id={"group": other},
                device_id_type=MESH,
            )
            copy.start()
            moves.append(copy)

    sph(
        table1, land1, nbr1, sends1, rho1, rho_s1, 2, blocks, lambda pick: pick,
        send_moving, keep,
    )

    code_copy.wait()
    for block in range(blocks):
        moved[block] = kept[block]
    finish(moves)
    for item in range(2 * halo):
        out2[item] = moved[code_s[sends2[0, item], 0]]
    second = exchange(out2, land2, 0, 4)
    for block in range(blocks):
        table2[block] = moved[code_s[block, 0]]
    prepare(kept, 0, blocks, 0)
    prepare(moved, blocks, moves_in, blocks)
    finish(second)

    def emit(block, state):
        for axis in range(3):
            pos_out[0, axis, pl.ds(block, 1), :] = state[axis : axis + 1]
            vel_out[0, axis, pl.ds(block, 1), :] = state[3 + axis : 4 + axis]
        rho_out[0, pl.ds(block, 1), :] = rho2[block]

    sph(
        table2, land2, nbr2, sends2, rho2, rho_s2, 6, blocks + moves_in,
        lambda pick: code_s[pick, 0],
        lambda pushed: None, emit,
    )


def body(
    n_curve, n_group,
    positions, velocities, masses, counts, neighbours_first, sends_first, new_slot,
    neighbours_second, sends_second,
):
    blocks, width = masses.shape[1], masses.shape[2]
    halo = sends_first.shape[1] // 2
    whole = blocks + 2 * halo
    peers = n_group - 1
    sources = neighbours_first.shape[2] + 1
    moves_in = MOVE_CAP * peers
    vmem = pl.BlockSpec(memory_space=pltpu.VMEM)
    places = [
        pltpu.VMEM((1, 3, blocks, width), F32),
        pltpu.VMEM((1, 3, blocks, width), F32),
        pltpu.VMEM(masses.shape, F32),
        pltpu.SMEM(counts.shape, jnp.int32),
        pltpu.SMEM((sources - 1, 1, blocks), jnp.int32),
        pltpu.SMEM(sends_first.shape, jnp.int32),
        pltpu.SMEM(new_slot.shape, jnp.int32),
        pltpu.VMEM(new_slot.shape, jnp.int32),
        pltpu.SMEM((sources - 1, 1, blocks), jnp.int32),
        pltpu.SMEM(sends_second.shape, jnp.int32),
        pltpu.SemaphoreType.DMA((10,)),
    ]
    scratch = places + [
        pltpu.VMEM((blocks, 8, width), F32),
        pltpu.VMEM((blocks, 8, width), F32),
        pltpu.VMEM((2 * halo, 8, width), F32),
        pltpu.VMEM((2 * halo, 8, width), F32),
        pltpu.VMEM((blocks, 8, width), F32),
        pltpu.VMEM((blocks + MOVE_CAP * peers, 8, width), F32),
        pltpu.VMEM((2 * halo, 8, width), F32),
        pltpu.VMEM((2 * halo, 8, width), F32),
        pltpu.VMEM((peers, MOVE_CAP, 8, width), F32),
        pltpu.VMEM((whole, 1, width), F32),
        pltpu.VMEM((whole, 1, width), F32),
        pltpu.VMEM((2 * halo, 1, width), F32),
        pltpu.VMEM((2 * halo, 1, width), F32),
        pltpu.VMEM((whole + moves_in, width, width), BF16),
        pltpu.VMEM((whole, 48, width), BF16),
        pltpu.VMEM((blocks + moves_in, width, 2 * width), BF16),
        pltpu.VMEM((whole, width, width), F32),
        pltpu.VMEM((whole + moves_in, width, width), F32),
        pltpu.VMEM((blocks, sources * width, width), BF16),
        pltpu.VMEM((blocks, sources * width, width), F32),
        pltpu.VMEM((1, width), jnp.int32),
        pltpu.VMEM((peers, 1, width), jnp.int32),
        pltpu.VMEM((whole, width), jnp.int32),
        pltpu.SMEM((whole, width), jnp.int32),
        pltpu.SemaphoreType.DMA((8,)),
        pltpu.SemaphoreType.DMA((8,)),
        pltpu.SemaphoreType.DMA((2 * peers,)),
        pltpu.SemaphoreType.DMA((2 * peers,)),
        pltpu.SemaphoreType.DMA,
    ]
    turned = jax.ShapeDtypeStruct((1, 3, blocks, width), F32)
    positions_out, velocities_out, densities_out = pl.pallas_call(
        functools.partial(kernel, n_curve, n_group),
        out_shape=(
            turned,
            turned,
            jax.ShapeDtypeStruct(masses.shape, F32),
        ),
        in_specs=[pl.BlockSpec(memory_space=pl.ANY)] * 9,
        out_specs=(vmem, vmem, vmem),
        scratch_shapes=scratch,
        compiler_params=pltpu.CompilerParams(
            collective_id=0, has_side_effects=True, vmem_limit_bytes=56 * 1024 * 1024
        ),
        name="sph",
    )(
        positions.transpose(0, 2, 1, 3), velocities.transpose(0, 2, 1, 3), masses, counts,
        neighbours_first.transpose(2, 0, 1), sends_first, new_slot,
        neighbours_second.transpose(2, 0, 1), sends_second,
    )
    return (
        positions_out.transpose(0, 2, 1, 3), velocities_out.transpose(0, 2, 1, 3), densities_out,
    )


def solution(mesh):
    blocks4 = P("group", "curve", None, None)
    blocks3 = P("group", "curve", None)
    blocks2 = P("group", "curve")
    in_specs = (
        blocks4, blocks4, blocks3, blocks2, blocks3, blocks2, blocks2, blocks3, blocks2,
    )
    return jax.shard_map(
        functools.partial(body, mesh.shape["curve"], mesh.shape["group"]),
        mesh=mesh, in_specs=in_specs, out_specs=(blocks4, blocks4, blocks3), check_vma=False,
    )
```
